128 devices in a mesh: fsdp: 16 (over x, y), grp: 8 (over z, core).
Axes of the slice: x: 4, y: 4, z: 4, core: 2. Of those that a mesh axis runs over, the one named last changes fastest.
Arguments:
- hidden: bfloat16 [1024, 32768], P(('fsdp', 'grp')), may hold values from -6 to 6
- grad_out: bfloat16 [1024, 7424], P(('fsdp', 'grp')), may hold values from -0.0048828125 to 0.0048828125
- token_counts: int32 [128], P(('fsdp', 'grp')), may hold values from 1 to 8
- weight: bfloat16 [32768, 7424], P(('fsdp', 'grp')), may hold values from -0.0546875 to 0.0546875
- old_mask: int32 [256, 58], P(('fsdp', 'grp')), may hold values from 0 to 1, as said below
- drop_list: int32 [128, 7], P(('fsdp', 'grp')), may hold values from 0 to 115, as said below
- grow_list: int32 [128, 7], P(('fsdp', 'grp')), may hold values from 0 to 115, as said below
- inputs: bfloat16 [1024, 32768], P('grp', 'fsdp'), may hold values from -6 to 6
Outputs:
- outputs: bfloat16 [1024, 7424], P('grp', 'fsdp')
- new_mask: int32 [256, 58], P(('fsdp', 'grp'))
The draws below stay inside these ranges and needn't reach their ends.
Inputs may be any that keep to these rules, and one draw needn't show every extreme that they name: `old_mask`: each owner keeps between 34 and 47 blocks, and some owner keeps exactly 47. `drop_list`: each owner's entries are distinct blocks that it keeps in old_mask. `grow_list`: each owner's entries are distinct blocks that it does not keep in old_mask.
All inputs are finite; a program needn't handle non-finite values.
Results may differ from the reference program's by a relative error of at most 0.02.
Values may be sent and summed in bfloat16 or wider, within the bound.
A program may use at most 128 MiB of HBM per device.

```python
import jax
import jax.numpy as jnp
from jax import lax

D = 7424
FFW = 32768
BLK = 128
TOK_DEV = 8
OWNERS = 128
TOKENS = 1024
FTOK = 1024
BR = 2
NBC = 58
FFB = 256
NB_DEV = 116
KMAX = 47
KLO = 34
NSWAP = 7
FSLAB = 2048
N_FSDP = 16
N_GRP = 8


def owner_layout(key):
    key_list = jax.random.split(key, OWNERS + 1)

    def draw_owner(owner_key, kept_count):
        shuffled = jax.random.permutation(owner_key, NB_DEV).astype(jnp.int32)
        position = jnp.zeros((NB_DEV,), jnp.int32).at[shuffled].set(jnp.arange(NB_DEV, dtype=jnp.int32))
        kept_flags = (position < kept_count).astype(jnp.int32)
        drop_ids = shuffled[:NSWAP]
        grow_ids = lax.dynamic_slice_in_dim(shuffled, kept_count, NSWAP)
        return (kept_flags, drop_ids, grow_ids)
    counts = jax.random.randint(key_list[0], (OWNERS,), KLO, KMAX + 1).astype(jnp.int32)
    full_owner = jax.random.randint(jax.random.fold_in(key_list[0], 7), (), 0, OWNERS)
    counts = counts.at[full_owner].set(KMAX)
    kept_all, drop_all, grow_all = jax.vmap(draw_owner)(key_list[1:], counts)
    return (kept_all.reshape(FFB, NBC), drop_all, grow_all)


def draw_old_mask(key, part):
    layout = owner_layout(key)
    return layout[0]


def draw_drop_list(key, part):
    layout = owner_layout(key)
    return layout[1]


def draw_grow_list(key, part):
    layout = owner_layout(key)
    return layout[2]


def with_ends(result, rng, smallest, top_value):
    place = [jax.random.randint(jax.random.fold_in(rng, axis), (), 0, length) for axis, length in enumerate(result.shape)]
    main_axis = result.shape.index(max(result.shape))
    next_to = place[:main_axis] + [(place[main_axis] + 1) % result.shape[main_axis]] + place[main_axis + 1:]
    return result.at[tuple(place)].set(smallest).at[tuple(next_to)].set(top_value)


def level_of(key, dims, cuts, low, top_value):
    gain = 1.0
    for axis_at, shards_of in cuts:
        steps = jax.random.uniform(jax.random.fold_in(jax.random.fold_in(key, 6), axis_at), (shards_of,), jnp.float32, low / len(cuts), top_value / len(cuts))
        gain = gain * jnp.repeat(jnp.exp(steps), dims[axis_at] // shards_of).reshape((-1,) + (1,) * (len(dims) - 1 - axis_at))
    return gain


def bell_draw(stream_key, shape, width, most, cuts=(), kind=jnp.bfloat16):
    values = jax.random.normal(stream_key, shape, jnp.float32) * width
    if len(cuts) > 0:
        values = level_of(stream_key, shape, cuts, -0.22, 0.18) * values
    return jnp.clip(values, min=-most, max=most).astype(kind)


def setup_inputs(seed: int = 0) -> dict:
    splits = jax.random.split(jax.random.key(seed), 9)
    return {
        "hidden": bell_draw(splits[0], (TOKENS, FFW), 1.0, 6.0, ((0, 128),)),
        "grad_out": bell_draw(splits[1], (TOKENS, D), (1.3 * (FFW * 2 // 5 * TOKENS) ** -0.5), 0.0048828125, ((0, 128),)),
        "token_counts": with_ends(jax.random.randint(splits[2], (OWNERS,), 1, TOK_DEV + 1), jax.random.fold_in(splits[2], 1), 1, TOK_DEV).astype(jnp.int32),
        "weight": bell_draw(splits[3], (FFW, D), (FFW * 2 // 5) ** -0.5, 0.0546875, ((0, 128),)),
        "old_mask": draw_old_mask(jax.random.fold_in(splits[8], 71), 0),
        "drop_list": draw_drop_list(jax.random.fold_in(splits[8], 71), 0),
        "grow_list": draw_grow_list(jax.random.fold_in(splits[8], 71), 0),
        "inputs": bell_draw(splits[7], (FTOK, FFW), 1.0, 6.0, ((0, 8), (1, 16))),
    }


def expand_mask(block_mask):
    return jnp.repeat(jnp.repeat(block_mask, BLK, axis=0), BLK, axis=1).astype(jnp.float32)


def reference(hidden, grad_out, token_counts, weight, old_mask, drop_list, grow_list, inputs):
    owners = N_FSDP * N_GRP
    token_ids = jnp.arange(TOKENS, dtype=jnp.int32)
    limits = jnp.repeat(token_counts, TOK_DEV)
    valid_rows = (token_ids % TOK_DEV) < limits
    masked_grad = jnp.where(valid_rows[:, None], grad_out, jnp.zeros_like(grad_out))
    flat_mask = old_mask.reshape(owners, BR * NBC)
    owner_ids = jnp.arange(owners, dtype=jnp.int32)[:, None]
    new_flat = flat_mask.at[owner_ids, drop_list].set(0).at[owner_ids, grow_list].set(1)
    new_mask = new_flat.reshape(FFB, NBC).astype(jnp.int32)
    slab_blocks = FSLAB // BLK

    def slab_pass(running, slab_index):
        first_col = (slab_index * FSLAB).astype(jnp.int32)
        first_block = (slab_index * slab_blocks).astype(jnp.int32)
        hid_slab = lax.dynamic_slice_in_dim(hidden, first_col, FSLAB, 1)
        slab_grad = lax.dot_general(hid_slab, masked_grad, (((0,), (0,)), ((), ())), preferred_element_type=jnp.float32)
        weight_slab = lax.dynamic_slice_in_dim(weight, first_col, FSLAB, 0)
        old_slab = lax.dynamic_slice_in_dim(old_mask, first_block, slab_blocks, 0)
        new_slab = lax.dynamic_slice_in_dim(new_mask, first_block, slab_blocks, 0)
        new_weight = (expand_mask(new_slab) * (expand_mask(old_slab) * weight_slab.astype(jnp.float32) - slab_grad)).astype(jnp.bfloat16)
        input_slab = lax.dynamic_slice_in_dim(inputs, first_col, FSLAB, 1)
        slab_out = jnp.dot(input_slab, new_weight, preferred_element_type=jnp.float32).astype(jnp.bfloat16)
        slab_out = lax.optimization_barrier(slab_out)
        return running + slab_out.astype(jnp.float32), None

    initial = jnp.zeros((FTOK, D), jnp.float32)
    summed, _ = lax.scan(slab_pass, initial, jnp.arange(N_FSDP, dtype=jnp.int32))
    return summed.astype(jnp.bfloat16), new_mask
```

```python
import jax
import jax.numpy as jnp
from jax import lax
from jax.experimental import pallas as pl
from jax.experimental.pallas import tpu as pltpu
from jax.sharding import PartitionSpec as P

MESH = pl.DeviceIdType.MESH
BF = jnp.bfloat16
F32 = jnp.float32

RING = 4
ROWS = 16
BLK = 128
HALF = 3712
OWN = 256
CHUNK = 464
PAD = 512

PARTS = ((0, 1280, 640), (1280, 1280, 640), (2560, 1152, 640))
GATHER = (("x", "y", "z"), ("y", "z", "x"), ("z", "x", "y"))
SCATTER = (("x", "y", "z"), ("y", "z", "x"), ("z", "x", "y"))
GDIMS = ("x", "y", "z")
SDIMS = ("z", "x", "y")


def pick(dims, fixed):
    return tuple(fixed[d] if d in fixed else slice(None) for d in dims)


def kernel(
    count_ref, drop_ref, grow_ref, old_ref, grad_ref, hid_ref, inp_ref, w_ref,
    out_ref, mask_ref,
    gm, gpar, g, h, ht, acc, w, xin, s, m, expand, ra1, rb1, ra2, rb2, ra3, rb3, fin, stage, land,
    g_send, g_recv, s_send, s_recv, e_send, e_recv, f_send, f_recv, loc,
):
    fsdp = lax.axis_index("fsdp")
    grp = lax.axis_index("grp")
    me = {"x": fsdp // RING, "y": fsdp % RING, "z": grp // 2}
    core = grp % 2

    def dev(x, y, z, c):
        return (x * RING + y, z * 2 + c)

    def near(axis, step):
        at = dict(me)
        at[axis] = (at[axis] + step) % RING
        return dev(at["x"], at["y"], at["z"], core)

    partner = dev(me["x"], me["y"], me["z"], 1 - core)

    mine = pl.ds(pl.multiple_of(core * HALF, BLK), HALF)
    other = pl.ds(pl.multiple_of((1 - core) * HALF, BLK), HALF)
    local = [
        pltpu.make_async_copy(w_ref.at[:, mine], w.at[pl.ds(0, OWN), :], loc.at[0]),
        pltpu.make_async_copy(hid_ref, h.at[0], loc.at[1]),
        pltpu.make_async_copy(inp_ref, xin.at[0], loc.at[2]),
    ]
    for c in local:
        c.start()

    bar = pltpu.get_barrier_semaphore()
    for axis in ("x", "y", "z"):
        for step in (1, -1):
            pl.semaphore_signal(bar, inc=1, device_id=near(axis, step), device_id_type=MESH)
    pl.semaphore_signal(bar, inc=1, device_id=partner, device_id_type=MESH)
    last_core = me["x"] // 2
    self_in = last_core == core
    own_k = (me["x"] % 2) * RING + me["y"]

    def last_dev(k):
        return dev(2 * core + k // RING, k % RING, me["z"], last_core)

    def is_self(k):
        return jnp.logical_and(self_in, own_k == k)

    for k in range(8):
        @pl.when(jnp.logical_not(is_self(k)))
        def _():
            pl.semaphore_signal(bar, inc=1, device_id=last_dev(k), device_id_type=MESH)

    rows = lax.broadcasted_iota(jnp.int32, grad_ref.shape, 0)
    gm[...] = jnp.where(rows < count_ref[0], grad_ref[...].astype(F32), 0.0).astype(BF)

    old = old_ref[...]
    ids = lax.broadcasted_iota(jnp.int32, old.shape, 0) * old.shape[1] + lax.broadcasted_iota(
        jnp.int32, old.shape, 1
    )
    new = old
    for k in range(drop_ref.shape[1]):
        new = jnp.where(ids == drop_ref[0, k], 0, new)
    for k in range(grow_ref.shape[1]):
        new = jnp.where(ids == grow_ref[0, k], 1, new)
    mask_ref[...] = new
    m[0] = jnp.zeros_like(m[0])
    m[0, 0:2, 0 : old.shape[1]] = new.astype(F32)
    m[0, 2:4, 0 : old.shape[1]] = (new * old).astype(F32)

    pl.semaphore_wait(bar, jnp.where(self_in, 14, 15))

    def remote(src, dst, sends, recvs, i, to):
        return pltpu.make_async_remote_copy(
            src_ref=src, dst_ref=dst, send_sem=sends.at[i], recv_sem=recvs.at[i],
            device_id=to, device_id_type=MESH,
        )

    swap = [
        remote(gm.at[:, other], gpar, e_send, e_recv, 0, partner),
        remote(m.at[0], m.at[1], e_send, e_recv, 1, partner),
        remote(hid_ref, h.at[1], e_send, e_recv, 2, partner),
        remote(w_ref.at[:, other], w.at[pl.ds(OWN, OWN), :], e_send, e_recv, 3, partner),
        remote(inp_ref, xin.at[1], e_send, e_recv, 4, partner),
    ]
    for c in swap:
        c.start()

    swap[0].wait_recv()
    a, b = gm[:, mine], gpar[...]
    first = core == 0
    g[me["x"], me["y"], me["z"]] = jnp.concatenate(
        [jnp.where(first, a, b), jnp.where(first, b, a)], axis=0
    )

    def gather_copy(p, q, j):
        off, width, half = PARTS[p]
        axis = GATHER[p][q]
        fixed = {d: me[d] for d in GATHER[p][q:]}
        if j == 0 or j == 1:
            cols = pl.ds(off, width)
            to = near(axis, 1 if j == 0 else -1)
        elif j == 2:
            fixed[axis] = (me[axis] - 1) % RING
            cols = pl.ds(off, half)
            to = near(axis, 1)
        else:
            fixed[axis] = (me[axis] + 1) % RING
            cols = pl.ds(off + half, width - half)
            to = near(axis, -1)
        ref = g.at[(*pick(GDIMS, fixed), slice(None), cols)]
        return remote(ref, ref, g_send, g_recv, (p * 3 + q) * 4 + j, to)

    gc = {(p, q, j): gather_copy(p, q, j) for p in range(3) for q in range(3) for j in range(4)}

    def tiles(p, body):
        off, width, _ = PARTS[p]
        whole = width // 256

        def step(t, carry):
            body(pl.multiple_of(off + t * 256, BLK), 256)
            return carry

        lax.fori_loop(0, whole, step, 0)
        if width % 256:
            body(off + whole * 256, width % 256)

    def grad_chunk(p, at, start):
        lhs = ht[p, at]
        sel = pick(GDIMS, {GATHER[p][2]: at})

        def body(o, n):
            rhs = g[(*sel, slice(None), pl.ds(o, n))].reshape(256, n)
            part = jnp.dot(lhs, rhs, preferred_element_type=F32)
            if start:
                acc[:, pl.ds(o, n)] = part
            else:
                acc[:, pl.ds(o, n)] += part

        tiles(p, body)

    for p in range(3):
        gc[p, 0, 0].start()
        gc[p, 0, 1].start()

    swap[1].wait_recv()

    def spread(t, carry):
        o = pl.multiple_of(t * BLK, BLK)
        block = lax.broadcasted_iota(jnp.int32, (BLK, BLK), 0) == core * (HALF // BLK) + t
        for i in range(2):
            expand[i, :, pl.ds(o, BLK)] = jnp.dot(
                m[i], block.astype(F32), preferred_element_type=F32
            )
        return carry

    def turn(i, carry):
        for p in range(3):
            sel = pick(GDIMS, {GATHER[p][2]: i})
            for side in range(2):
                part = h[(side, *sel)].reshape(256, OWN)
                ht[p, i, pl.ds(side * OWN, OWN), :] = part.T
        return carry

    for q in range(3):
        for p in range(3):
            gc[p, q, 0].wait_recv()
            gc[p, q, 2].start()
            gc[p, q, 1].wait_recv()
            gc[p, q, 3].start()
            if q == 2:
                axis = GATHER[p][2]
                grad_chunk(p, (me[axis] + 3) % RING, False)
                grad_chunk(p, (me[axis] + 1) % RING, False)
        if q == 0:
            lax.fori_loop(0, HALF // BLK, spread, 0)
        if q < 2:
            for p in range(3):
                gc[p, q, 2].wait_recv()
                gc[p, q, 3].wait_recv()
                gc[p, q + 1, 0].start()
                gc[p, q + 1, 1].start()
        if q == 0:
            local[1].wait()
            swap[2].wait_recv()
            lax.fori_loop(0, RING, turn, 0)
        if q == 1:
            for p in range(3):
                grad_chunk(p, me[GATHER[p][2]], True)
            local[0].wait()
            swap[3].wait_recv()
            local[2].wait()
            swap[4].wait_recv()

    ras, rbs = (ra1, ra2, ra3), (rb1, rb2, rb3)

    def scatter_copy(p, q, j):
        off, width, half = PARTS[p]
        axis = SCATTER[p][q]
        fixed = {d: me[d] for d in SCATTER[p][:q]}
        lo, hi = pl.ds(off, half), pl.ds(off + half, width - half)
        step = 1 if j % 2 == 0 else -1
        if j < 2:
            fixed[axis] = (me[axis] + 2) % RING
            cols = lo if j == 0 else hi
            into = ras[q]
        else:
            fixed[axis] = (me[axis] + step) % RING
            cols = (hi, lo, lo, hi)[j - 2]
            into = rbs[q].at[j % 2]
        src = s.at[(*pick(SDIMS, fixed), slice(None), cols)]
        dst = into.at[(*([slice(None)] * (3 - q)), cols)]
        return remote(src, dst, s_send, s_recv, (p * 3 + q) * 6 + j, near(axis, step))

    sc = {(p, q, j): scatter_copy(p, q, j) for p in range(3) for q in range(3) for j in range(6)}

    def out_chunk(p, at):
        sel = pick(SDIMS, {SCATTER[p][0]: at})
        left = xin[(0, *sel)].reshape(256, OWN)
        right = xin[(1, *sel)].reshape(256, OWN)

        def body(o, n):
            cols = pl.ds(o, n)
            part = jnp.dot(left, w[0:OWN, cols], preferred_element_type=F32)
            part = part + jnp.dot(right, w[OWN : 2 * OWN, cols], preferred_element_type=F32)
            s[(*sel, slice(None), cols)] = part.astype(BF).reshape(RING, RING, ROWS, n)

        tiles(p, body)

    def update(p):
        def body(o, n):
            cols = pl.ds(o, n)
            for r in range(4):
                side, row = r // 2, r % 2
                keep = expand[side, row : row + 1, cols]
                both = expand[side, row + 2 : row + 3, cols]
                span = pl.ds(r * BLK, BLK)
                w[span, cols] = (both * w[span, cols].astype(F32) - keep * acc[span, cols]).astype(BF)

        tiles(p, body)

    for p in range(3):
        gc[p, 2, 2].wait_recv()
        gc[p, 2, 3].wait_recv()
        axis = SCATTER[p][0]
        grad_chunk(p, (me[GATHER[p][2]] + 2) % RING, False)
        update(p)
        out_chunk(p, (me[axis] + 2) % RING)
        sc[p, 0, 0].start()
        sc[p, 0, 1].start()
    for p in range(3):
        axis = SCATTER[p][0]
        out_chunk(p, (me[axis] + 1) % RING)
        sc[p, 0, 2].start()
        out_chunk(p, (me[axis] + 3) % RING)
        sc[p, 0, 3].start()

    def add_into(p, q, v, cols, froms):
        fixed = {d: me[d] for d in SCATTER[p][:q]}
        fixed[SCATTER[p][q]] = v
        free = [d for d in SDIMS if d not in fixed]

        def one(lead):
            idx = dict(fixed)
            if free:
                idx[free[0]] = lead
            at = (*pick(SDIMS, idx), slice(None), cols)
            there = ((lead,) if free else ()) + (slice(None),) * (len(free) - 1 if free else 0)
            total = s[at].astype(F32)
            for ref, pre in froms:
                total = total + ref[(*pre, *there, slice(None), cols)].astype(F32)
            return at, total

        if not free:
            return one(None)

        def step(i, carry):
            at, total = one(i)
            s[at] = total.astype(BF)
            return carry

        lax.fori_loop(0, RING, step, 0)
        return None

    def store(done):
        if done is not None:
            s[done[0]] = done[1].astype(BF)

    for q in range(3):
        for p in range(3):
            off, width, half = PARTS[p]
            lo, hi = pl.ds(off, half), pl.ds(off + half, width - half)
            axis = SCATTER[p][q]
            sc[p, q, 0].wait_recv()
            store(add_into(p, q, (me[axis] + 1) % RING, lo, [(ras[q], ())]))
            sc[p, q, 4].start()
            sc[p, q, 1].wait_recv()
            store(add_into(p, q, (me[axis] + 3) % RING, hi, [(ras[q], ())]))
            sc[p, q, 5].start()
        for p in range(3):
            off, width, half = PARTS[p]
            axis = SCATTER[p][q]
            if q == 0:
                out_chunk(p, me[axis])
        for p in range(3):
            off, width, half = PARTS[p]
            axis = SCATTER[p][q]
            for j in (2, 3, 4, 5):
                sc[p, q, j].wait_recv()
            done = add_into(
                p, q, me[axis], pl.ds(off, width), [(rbs[q], (0,)), (rbs[q], (1,))]
            )
            if q < 2:
                for j in range(4):
                    sc[p, q + 1, j].start()
            else:
                fin[:, pl.ds(off, width)] = done[1]

    fin[:, pl.ds(HALF, BLK)] = jnp.zeros((ROWS, BLK), F32)
    slot = fsdp % 8
    ends = []
    for k in range(8):
        base, shift = CHUNK * k // BLK * BLK, CHUNK * k % BLK
        piece = fin[:, pl.ds(base, PAD + BLK)]
        if shift:
            piece = pltpu.roll(piece, PAD + BLK - shift, 1)
        stage[k] = piece[:, :PAD].astype(BF)
        far = pltpu.make_async_remote_copy(
            src_ref=stage.at[k], dst_ref=land.at[slot], send_sem=f_send.at[k],
            recv_sem=f_recv.at[slot], device_id=last_dev(k), device_id_type=MESH,
        )
        near_copy = pltpu.make_async_copy(stage.at[k], land.at[slot], f_recv.at[slot])

        @pl.when(jnp.logical_not(is_self(k)))
        def _():
            far.start()

        @pl.when(is_self(k))
        def _():
            near_copy.start()

        ends.append(far)
    for k in range(8):
        pltpu.make_async_copy(stage.at[k], land.at[k], f_recv.at[k]).wait()
        out_ref[pl.ds(k * ROWS, ROWS), :] = land[k][:, :CHUNK]

    for k in range(8):
        @pl.when(jnp.logical_not(is_self(k)))
        def _():
            ends[k].wait_send()
    for c in swap:
        c.wait_send()
    for c in gc.values():
        c.wait_send()
    for c in sc.values():
        c.wait_send()


def shards(hidden, grad_out, token_counts, weight, old_mask, drop_list, grow_list, inputs):
    sections = hidden.reshape(8, 128, OWN)
    hid = lax.all_to_all(sections, ("fsdp", "grp"), split_axis=1, concat_axis=0, tiled=True)
    hid = hid.reshape(RING, RING, RING, ROWS, OWN)
    inp = lax.all_to_all(
        inputs.reshape(128, 8, OWN), "grp", split_axis=1, concat_axis=0, tiled=True
    ).reshape(RING, RING, RING, ROWS, OWN)
    vmem = pl.BlockSpec(memory_space=pltpu.VMEM)
    smem = pl.BlockSpec(memory_space=pltpu.SMEM)
    hbm = pl.BlockSpec(memory_space=pl.ANY)
    dma = pltpu.SemaphoreType.DMA
    cube = (RING, RING, RING, ROWS)
    out, mask = pl.pallas_call(
        kernel,
        out_shape=(
            jax.ShapeDtypeStruct((128, CHUNK), BF),
            jax.ShapeDtypeStruct(old_mask.shape, jnp.int32),
        ),
        in_specs=[smem, smem, smem, vmem, vmem, hbm, hbm, hbm],
        out_specs=(vmem, vmem),
        scratch_shapes=[
            pltpu.VMEM((8, 2 * HALF), BF),
            pltpu.VMEM((8, HALF), BF),
            pltpu.VMEM((*cube, HALF), BF),
            pltpu.VMEM((2, *cube, OWN), BF),
            pltpu.VMEM((3, RING, 2 * OWN, 256), BF),
            pltpu.VMEM((2 * OWN, HALF), F32),
            pltpu.VMEM((2 * OWN, HALF), BF),
            pltpu.VMEM((2, *cube, OWN), BF),
            pltpu.VMEM((*cube, HALF), BF),
            pltpu.VMEM((2, 8, BLK), F32),
            pltpu.VMEM((2, 8, HALF), F32),
            pltpu.VMEM((RING, RING, ROWS, HALF), BF),
            pltpu.VMEM((2, RING, RING, ROWS, HALF), BF),
            pltpu.VMEM((RING, ROWS, HALF), BF),
            pltpu.VMEM((2, RING, ROWS, HALF), BF),
            pltpu.VMEM((ROWS, HALF), BF),
            pltpu.VMEM((2, ROWS, HALF), BF),
            pltpu.VMEM((ROWS, HALF + BLK), F32),
            pltpu.VMEM((8, ROWS, PAD), BF),
            pltpu.VMEM((8, ROWS, PAD), BF),
            dma((36,)), dma((36,)), dma((54,)), dma((54,)), dma((5,)), dma((5,)),
            dma((8,)), dma((8,)), dma((3,)),
        ],
        compiler_params=pltpu.CompilerParams(
            collective_id=0, has_side_effects=True, vmem_limit_bytes=60 * 2**20
        ),
        cost_estimate=pl.CostEstimate(flops=8 * 10**9, bytes_accessed=10**7, transcendentals=0),
    )(token_counts, drop_list, grow_list, old_mask, grad_out, hid, inp, weight)
    return (out, mask)


def solution(mesh):
    split = P(("fsdp", "grp"), None)
    return jax.shard_map(
        shards,
        mesh=mesh,
        in_specs=(split, split, P(("fsdp", "grp")), split, split, split, split, P("grp", "fsdp")),
        out_specs=(P("grp", "fsdp"), split),
        check_vma=False,
    )
```

```python
import jax
import jax.numpy as jnp
from jax import lax
from jax.experimental import pallas as pl
from jax.experimental.pallas import tpu as pltpu
from jax.sharding import PartitionSpec as P

MESH = pl.DeviceIdType.MESH
BF = jnp.bfloat16
F32 = jnp.float32

RING = 4
ROWS = 16
BLK = 128
HALF = 3712
OWN = 256
CHUNK = 464
PAD = 512

PARTS = (
    ((0, 640, 384), (640, 512, 256)),
    ((1152, 768, 384), (1920, 512, 256)),
    ((2432, 768, 384), (3200, 512, 256)),
)
GROUPS = 2
FAR = (1, 3, 2)
GATHER = (("x", "y", "z"), ("y", "z", "x"), ("z", "x", "y"))
SCATTER = (("x", "y", "z"), ("y", "z", "x"), ("z", "x", "y"))
GDIMS = ("x", "y", "z")
SDIMS = ("z", "x", "y")


def pick(dims, fixed):
    return tuple(fixed[d] if d in fixed else slice(None) for d in dims)


def kernel(
    count_ref, drop_ref, grow_ref, old_ref, grad_ref, hid_ref, inp_ref, w_ref,
    out_ref, mask_ref,
    count, drop, grow, old_v, grad, gm, gp, g, hb, t0, t1, t2, h, ht, acc, w, xin, s, m, expand, ra1, rb1, rb2, rb3, fin, stage, land,
    g_send, g_recv, s_send, s_recv, e_send, e_recv, f_send, f_recv, a_send, a_recv, loc,
):
    fsdp = lax.axis_index("fsdp")
    grp = lax.axis_index("grp")
    me = {"x": fsdp // RING, "y": fsdp % RING, "z": grp // 2}
    core = grp % 2

    def dev(x, y, z, c):
        return (x * RING + y, z * 2 + c)

    def near(axis, step):
        at = dict(me)
        at[axis] = (at[axis] + step) % RING
        return dev(at["x"], at["y"], at["z"], core)

    partner = dev(me["x"], me["y"], me["z"], 1 - core)

    bar = pltpu.get_barrier_semaphore()
    last_core = me["x"] // 2
    self_in = last_core == core
    own_k = (me["x"] % 2) * RING + me["y"]

    def last_dev(k):
        return dev(2 * core + k // RING, k % RING, me["z"], last_core)

    def is_self(k):
        return jnp.logical_and(self_in, own_k == k)

    for axis in ("x", "y", "z"):
        for step in FAR:
            pl.semaphore_signal(bar, inc=1, device_id=near(axis, step), device_id_type=MESH)
    pl.semaphore_signal(bar, inc=1, device_id=partner, device_id_type=MESH)
    for k in range(8):
        @pl.when(jnp.logical_not(is_self(k)))
        def _():
            pl.semaphore_signal(bar, inc=1, device_id=last_dev(k), device_id_type=MESH)

    mine = pl.ds(pl.multiple_of(core * HALF, BLK), HALF)
    other = pl.ds(pl.multiple_of((1 - core) * HALF, BLK), HALF)
    own_rows = pl.ds(pl.multiple_of(core * OWN, OWN), OWN)
    own_tokens = pl.ds(2 * core, 2)

    def slab(z):
        return pl.ds(pl.multiple_of(z * 2 * OWN, 2 * OWN), 2 * OWN)

    local = [
        pltpu.make_async_copy(*pair, loc.at[i])
        for i, pair in enumerate((
            (grad_ref, grad),
            (count_ref, count),
            (hid_ref, hb.at[core]),
            (old_ref, old_v),
            (drop_ref, drop),
            (grow_ref, grow),
            (w_ref.at[:, mine], w.at[own_rows, :]),
            (inp_ref.at[:, :, :, slab(me["z"])], xin.at[me["z"], own_tokens]),
        ))
    ]
    for c in local:
        c.start()

    def remote(src, dst, sends, recvs, i, to):
        return pltpu.make_async_remote_copy(
            src_ref=src, dst_ref=dst, send_sem=sends.at[i], recv_sem=recvs.at[i],
            device_id=to, device_id_type=MESH,
        )

    local[0].wait()
    local[1].wait()
    rows = lax.broadcasted_iota(jnp.int32, grad.shape, 0)
    gm[...] = jnp.where(rows < count[0], grad[...].astype(F32), 0.0).astype(BF)
    gp[core] = gm[:, mine]
    pl.semaphore_wait(bar, jnp.where(self_in, 17, 18))

    swap = [
        remote(gm.at[:, other], gp.at[core], e_send, e_recv, 0, partner),
        remote(hid_ref, hb.at[core], e_send, e_recv, 1, partner),
        remote(m.at[core], m.at[core], e_send, e_recv, 2, partner),
        remote(w_ref.at[:, other], w.at[own_rows, :], e_send, e_recv, 3, partner),
        remote(h.at[core], h.at[core], e_send, e_recv, 4, partner),
        remote(xin.at[:, own_tokens], xin.at[:, own_tokens], e_send, e_recv, 5, partner),
    ]
    swap[0].start()
    swap[1].start()
    swap[3].start()

    inp = [
        remote(
            inp_ref.at[:, :, :, slab((me["z"] + d) % RING)], xin.at[me["z"], own_tokens],
            a_send, a_recv, i, near("z", d),
        )
        for i, d in enumerate(FAR)
    ]
    def hid_step(axis, d):
        v = (me[axis] + d) % RING
        return {
            "x": (t0.at[v], t1.at[me["x"]]),
            "y": (t1.at[:, v], t2.at[:, me["y"]]),
            "z": (t2.at[:, :, v], h.at[core, :, :, me["z"]]),
        }[axis]

    hid = {}
    for q, axis in enumerate(("x", "y", "z")):
        stay = pltpu.make_async_copy(*hid_step(axis, 0), loc.at[8 + q])
        go = [
            remote(*hid_step(axis, d), a_send, a_recv, 3 + q * 3 + i, near(axis, d))
            for i, d in enumerate(FAR)
        ]
        hid[axis] = (stay, go)

    def hid_start(axis):
        for c in (*hid[axis][1], hid[axis][0]):
            c.start()

    def hid_wait(axis):
        hid[axis][0].wait()
        for c in hid[axis][1]:
            c.wait_recv()

    swap[0].wait_recv()
    g[me["x"], me["y"], me["z"]] = jnp.concatenate([gp[0], gp[1]], axis=0)

    sends = []

    def gather_copy(p, q, cols, at, to):
        fixed = {d: me[d] for d in GATHER[p][q:]}
        fixed[GATHER[p][q]] = at
        ref = g.at[(*pick(GDIMS, fixed), slice(None), cols)]
        sends.append(remote(ref, ref, g_send, g_recv, len(sends), to))
        return sends[-1]

    def gather_direct(p, q):
        axis = GATHER[p][q]
        cols = pl.ds(PARTS[p][0][0], sum(n for _, n, _ in PARTS[p]))
        return [gather_copy(p, q, cols, me[axis], near(axis, d)) for d in FAR]

    def gather_ring(p, q, off, width, half):
        axis = GATHER[p][q]
        cols, lo, hi = pl.ds(off, width), pl.ds(off, half), pl.ds(off + half, width - half)
        return [
            gather_copy(p, q, cols, me[axis], near(axis, 1)),
            gather_copy(p, q, cols, me[axis], near(axis, 3)),
            gather_copy(p, q, lo, (me[axis] + 3) % RING, near(axis, 1)),
            gather_copy(p, q, hi, (me[axis] + 1) % RING, near(axis, 3)),
        ]

    g0 = [gather_direct(p, 0) for p in range(3)]
    g1 = [gather_direct(p, 1) for p in range(3)]
    g2 = [[gather_ring(p, 2, *PARTS[p][k]) for p in range(3)] for k in range(GROUPS)]

    def start(copies):
        for c in copies:
            c.start()

    def arrive(copies):
        for c in copies:
            c.wait_recv()

    def tiles(p, k, body):
        off, width, _ = PARTS[p][k]
        whole = width // 256

        def step(t, carry):
            body(pl.multiple_of(off + t * 256, BLK), 256)
            return carry

        lax.fori_loop(0, whole, step, 0)
        if width % 256:
            body(off + whole * 256, width % 256)

    def grad_chunk(p, k, step):
        axis = GATHER[p][2]
        at = (me[axis] + step) % RING
        lhs = ht[p, at]
        sel = pick(GDIMS, {axis: at})

        def body(o, n):
            rhs = g[(*sel, slice(None), pl.ds(o, n))].reshape(256, n)
            part = jnp.dot(lhs, rhs, preferred_element_type=F32)
            if step == 0:
                acc[:, pl.ds(o, n)] = part
            else:
                acc[:, pl.ds(o, n)] += part

        tiles(p, k, body)

    for p in range(3):
        start(g0[p])

    for c in local[3:6]:
        c.wait()
    old = old_v[...]
    ids = lax.broadcasted_iota(jnp.int32, old.shape, 0) * old.shape[1] + lax.broadcasted_iota(
        jnp.int32, old.shape, 1
    )
    new = old
    for i in range(drop.shape[1]):
        new = jnp.where(ids == drop[0, i], 0, new)
    for i in range(grow.shape[1]):
        new = jnp.where(ids == grow[0, i], 1, new)
    mask_ref[...] = new
    m[core] = jnp.zeros((8, BLK), F32)
    m[core, 0:2, 0 : old.shape[1]] = new.astype(F32)
    m[core, 2:4, 0 : old.shape[1]] = (new * old).astype(F32)
    swap[2].start()

    local[2].wait()
    swap[1].wait_recv()

    def sort_hidden(j, carry):
        cols = pl.ds(pl.multiple_of(j * 2 * OWN + core * OWN, OWN), OWN)
        t0[j // 16, j // 4 % 4, j % 4] = jnp.concatenate([hb[0, :, cols], hb[1, :, cols]], axis=0)
        return carry

    lax.fori_loop(0, 64, sort_hidden, 0)
    hid_start("x")
    start(inp)

    def spread(t, carry):
        o = pl.multiple_of(t * BLK, BLK)
        block = lax.broadcasted_iota(jnp.int32, (BLK, BLK), 0) == core * (HALF // BLK) + t
        for i in range(2):
            expand[i, :, pl.ds(o, BLK)] = jnp.dot(
                m[i], block.astype(F32), preferred_element_type=F32
            )
        return carry

    def turn(i, carry):
        for p in range(3):
            sel = pick(GDIMS, {GATHER[p][2]: i})
            for side in range(2):
                part = h[(side, *sel)].reshape(256, OWN)
                ht[p, i, pl.ds(side * OWN, OWN), :] = part.T
        return carry

    for p in range(3):
        arrive(g0[p])
        start(g1[p])
    swap[2].wait_recv()
    lax.fori_loop(0, HALF // BLK, spread, 0)
    hid_wait("x")
    hid_start("y")
    for p in range(3):
        arrive(g1[p])
        start(g2[0][p][:2])
    hid_wait("y")
    hid_start("z")
    local[7].wait()
    arrive(inp)
    swap[5].start()
    hid_wait("z")
    swap[4].start()
    swap[4].wait_recv()
    lax.fori_loop(0, RING, turn, 0)
    for p in range(3):
        for k in range(GROUPS):
            grad_chunk(p, k, 0)
    local[6].wait()
    swap[3].wait_recv()
    swap[5].wait_recv()

    posts = []

    def scatter_copy(p, q, v, cols, into, to):
        fixed = {d: me[d] for d in SCATTER[p][:q]}
        fixed[SCATTER[p][q]] = v
        src = s.at[(*pick(SDIMS, fixed), slice(None), cols)]
        dst = into.at[(*([slice(None)] * (3 - q)), cols)]
        posts.append(remote(src, dst, s_send, s_recv, len(posts), to))
        return posts[-1]

    def scatter_ring(p, off, width, half):
        axis = SCATTER[p][0]
        lo, hi = pl.ds(off, half), pl.ds(off + half, width - half)
        out = []
        for step, cols in ((1, lo), (3, hi)):
            out.append(scatter_copy(p, 0, (me[axis] + 2) % RING, cols, ra1, near(axis, step)))
        for i, (step, cols) in enumerate(((1, hi), (3, lo), (1, lo), (3, hi))):
            v = (me[axis] + step) % RING
            out.append(scatter_copy(p, 0, v, cols, rb1.at[i % 2], near(axis, step)))
        return out

    def scatter_direct(p, q, off, width, half):
        axis = SCATTER[p][q]
        into = (rb2, rb3)[q - 1]
        return [
            scatter_copy(p, q, (me[axis] + d) % RING, pl.ds(off, width), into.at[i], near(axis, d))
            for i, d in enumerate(FAR)
        ]

    s0 = [[scatter_ring(p, *PARTS[p][k]) for p in range(3)] for k in range(GROUPS)]
    s1 = [[scatter_direct(p, 1, *PARTS[p][k]) for p in range(3)] for k in range(GROUPS)]
    s2 = [[scatter_direct(p, 2, *PARTS[p][k]) for p in range(3)] for k in range(GROUPS)]

    def out_chunk(p, k, step):
        axis = SCATTER[p][0]
        sel = pick(SDIMS, {axis: (me[axis] + step) % RING})
        lhs = xin[sel].reshape(256, 2 * OWN)

        def body(o, n):
            cols = pl.ds(o, n)
            part = jnp.dot(lhs, w[:, cols], preferred_element_type=F32)
            s[(*sel, slice(None), cols)] = part.astype(BF).reshape(RING, RING, ROWS, n)

        tiles(p, k, body)

    def update(p, k):
        def body(o, n):
            cols = pl.ds(o, n)
            for r in range(4):
                side, row = r // 2, r % 2
                keep = expand[side, row : row + 1, cols]
                both = expand[side, row + 2 : row + 3, cols]
                span = pl.ds(r * BLK, BLK)
                w[span, cols] = (both * w[span, cols].astype(F32) - keep * acc[span, cols]).astype(BF)

        tiles(p, k, body)

    def add_into(p, q, v, cols, froms):
        fixed = {d: me[d] for d in SCATTER[p][:q]}
        fixed[SCATTER[p][q]] = v
        free = [d for d in SDIMS if d not in fixed]

        def one(lead):
            idx = dict(fixed)
            if free:
                idx[free[0]] = lead
            at = (*pick(SDIMS, idx), slice(None), cols)
            there = ((lead,) if free else ()) + (slice(None),) * (len(free) - 1 if free else 0)
            total = s[at].astype(F32)
            for ref, pre in froms:
                total = total + ref[(*pre, *there, slice(None), cols)].astype(F32)
            return at, total

        if not free:
            return one(None)[1]

        def step(i, carry):
            at, total = one(i)
            s[at] = total.astype(BF)
            return carry

        lax.fori_loop(0, RING, step, 0)
        return None

    def finish(k):
        for p in range(3):
            arrive(g2[k][p][2:])
            grad_chunk(p, k, 2)
            update(p, k)
            out_chunk(p, k, 2)
            start(s0[k][p][:2])

    def sides(k):
        for p in range(3):
            out_chunk(p, k, 1)
            s0[k][p][2].start()
            out_chunk(p, k, 3)
            s0[k][p][3].start()

    def relay(k):
        for p in range(3):
            off, width, half = PARTS[p][k]
            for i, cols in enumerate((pl.ds(off, half), pl.ds(off + half, width - half))):
                s0[k][p][i].wait_recv()
                add_into(p, 0, (me[SCATTER[p][0]] + (1, 3)[i]) % RING, cols, [(ra1, ())])
                s0[k][p][4 + i].start()

    def settle(k):
        for p in range(3):
            off, width, _ = PARTS[p][k]
            arrive(s0[k][p][2:])
            add_into(p, 0, me[SCATTER[p][0]], pl.ds(off, width), [(rb1, (0,)), (rb1, (1,))])
            start(s1[k][p])

    for p in range(3):
        arrive(g2[0][p][:2])
        start(g2[0][p][2:])
        start(g2[1][p][:2])
    for p in range(3):
        grad_chunk(p, 0, 1)
        grad_chunk(p, 0, 3)
    finish(0)
    for p in range(3):
        arrive(g2[1][p][:2])
        start(g2[1][p][2:])
    sides(0)
    for p in range(3):
        grad_chunk(p, 1, 1)
        grad_chunk(p, 1, 3)
    relay(0)
    finish(1)
    sides(1)
    for k in range(GROUPS):
        for p in range(3):
            out_chunk(p, k, 0)
    relay(1)
    settle(0)
    settle(1)
    for k in range(GROUPS):
        for p in range(3):
            off, width, _ = PARTS[p][k]
            arrive(s1[k][p])
            add_into(p, 1, me[SCATTER[p][1]], pl.ds(off, width), [(rb2, (i,)) for i in range(3)])
            start(s2[k][p])
    for k in range(GROUPS):
        for p in range(3):
            off, width, _ = PARTS[p][k]
            arrive(s2[k][p])
            total = add_into(p, 2, me[SCATTER[p][2]], pl.ds(off, width), [(rb3, (i,)) for i in range(3)])
            fin[:, pl.ds(off, width)] = total

    fin[:, pl.ds(HALF, BLK)] = jnp.zeros((ROWS, BLK), F32)
    slot = fsdp % 8
    ends = []
    for k in range(8):
        base, shift = CHUNK * k // BLK * BLK, CHUNK * k % BLK
        piece = fin[:, pl.ds(base, PAD + BLK)]
        if shift:
            piece = pltpu.roll(piece, PAD + BLK - shift, 1)
        stage[k] = piece[:, :PAD].astype(BF)
        away = pltpu.make_async_remote_copy(
            src_ref=stage.at[k], dst_ref=land.at[slot], send_sem=f_send.at[k],
            recv_sem=f_recv.at[slot], device_id=last_dev(k), device_id_type=MESH,
        )
        near_copy = pltpu.make_async_copy(stage.at[k], land.at[slot], f_recv.at[slot])

        @pl.when(jnp.logical_not(is_self(k)))
        def _():
            away.start()

        @pl.when(is_self(k))
        def _():
            near_copy.start()

        ends.append(away)
    for k in range(8):
        pltpu.make_async_copy(stage.at[k], land.at[k], f_recv.at[k]).wait()
        out_ref[pl.ds(k * ROWS, ROWS), :] = land[k][:, :CHUNK]

    for k in range(8):
        @pl.when(jnp.logical_not(is_self(k)))
        def _():
            ends[k].wait_send()
    for c in swap:
        c.wait_send()
    for c in (*sends, *posts):
        c.wait_send()
    for c in (*inp, *hid["x"][1], *hid["y"][1], *hid["z"][1]):
        c.wait_send()


def shards(hidden, grad_out, token_counts, weight, old_mask, drop_list, grow_list, inputs):
    inp = inputs.reshape(2, RING, ROWS, 2048)
    vmem = pl.BlockSpec(memory_space=pltpu.VMEM)
    hbm = pl.BlockSpec(memory_space=pl.ANY)
    dma = pltpu.SemaphoreType.DMA
    cube = (RING, RING, RING, ROWS)
    out, mask = pl.pallas_call(
        kernel,
        out_shape=(
            jax.ShapeDtypeStruct((128, CHUNK), BF),
            jax.ShapeDtypeStruct(old_mask.shape, jnp.int32),
        ),
        in_specs=[hbm] * 8,
        out_specs=(vmem, vmem),
        scratch_shapes=[
            pltpu.SMEM((1,), jnp.int32),
            pltpu.SMEM(drop_list.shape, jnp.int32),
            pltpu.SMEM(grow_list.shape, jnp.int32),
            pltpu.VMEM(old_mask.shape, jnp.int32),
            pltpu.VMEM((8, 2 * HALF), BF),
            pltpu.VMEM((8, 2 * HALF), BF),
            pltpu.VMEM((2, 8, HALF), BF),
            pltpu.VMEM((*cube, HALF), BF),
            pltpu.VMEM((2, 8, 64 * 2 * OWN), BF),
            pltpu.VMEM((*cube, OWN), BF),
            pltpu.VMEM((*cube, OWN), BF),
            pltpu.VMEM((*cube, OWN), BF),
            pltpu.VMEM((2, *cube, OWN), BF),
            pltpu.VMEM((3, RING, 2 * OWN, 256), BF),
            pltpu.VMEM((2 * OWN, HALF), F32),
            pltpu.VMEM((2 * OWN, HALF), BF),
            pltpu.VMEM((*cube, 2 * OWN), BF),
            pltpu.VMEM((*cube, HALF), BF),
            pltpu.VMEM((2, 8, BLK), F32),
            pltpu.VMEM((2, 8, HALF), F32),
            pltpu.VMEM((RING, RING, ROWS, HALF), BF),
            pltpu.VMEM((2, RING, RING, ROWS, HALF), BF),
            pltpu.VMEM((3, RING, ROWS, HALF), BF),
            pltpu.VMEM((3, ROWS, HALF), BF),
            pltpu.VMEM((ROWS, HALF + BLK), F32),
            pltpu.VMEM((8, ROWS, PAD), BF),
            pltpu.VMEM((8, ROWS, PAD), BF),
            dma((42,)), dma((42,)), dma((72,)), dma((72,)), dma((6,)), dma((6,)),
            dma((8,)), dma((8,)), dma((12,)), dma((12,)), dma((11,)),
        ],
        compiler_params=pltpu.CompilerParams(
            collective_id=0, has_side_effects=True, vmem_limit_bytes=60 * 2**20
        ),
        cost_estimate=pl.CostEstimate(flops=8 * 10**9, bytes_accessed=10**7, transcendentals=0),
    )(token_counts, drop_list, grow_list, old_mask, grad_out, hidden, inp, weight)
    return (out, mask)


def solution(mesh):
    split = P(("fsdp", "grp"), None)
    return jax.shard_map(
        shards,
        mesh=mesh,
        in_specs=(split, split, P(("fsdp", "grp")), split, split, split, split, P("grp", "fsdp")),
        out_specs=(P("grp", "fsdp"), split),
        check_vma=False,
    )
```

```python
import jax
import jax.numpy as jnp
from jax import lax
from jax.experimental import pallas as pl
from jax.experimental.pallas import tpu as pltpu
from jax.sharding import PartitionSpec as P

MESH = pl.DeviceIdType.MESH
BF = jnp.bfloat16
F32 = jnp.float32

RING = 4
ROWS = 16
BLK = 128
HALF = 3712
OWN = 256
CHUNK = 464
PAD = 512

PARTS = (
    ((0, 640, 384), (2176, 512, 256)),
    ((640, 768, 384), (2688, 512, 256)),
    ((1408, 768, 384), (3200, 512, 256)),
)
GROUPS = 2
FAR = (1, 3, 2)
TURNS = (("x", "y", "z"), ("y", "z", "x"))
GATHER = (("x", "y", "z"), ("y", "z", "x"), ("z", "x", "y"))
SCATTER = (("x", "y", "z"), ("y", "z", "x"), ("z", "x", "y"))
GDIMS = ("x", "y", "z")
SDIMS = ("z", "x", "y")


def pick(dims, fixed):
    return tuple(fixed[d] if d in fixed else slice(None) for d in dims)


def kernel(
    count_ref, drop_ref, grow_ref, old_ref, grad_ref, hid_ref, inp_ref, w_ref,
    out_ref, mask_ref,
    count, drop, grow, old_v, grad, gm, gp, g, hb, t0, t1, t2, h, ht, acc, w, xin, s, m, expand, ra1, rb1, rb2, rb3, fin, stage, land,
    g_send, g_recv, s_send, s_recv, e_send, e_recv, f_send, f_recv, a_send, a_recv, loc,
):
    fsdp = lax.axis_index("fsdp")
    grp = lax.axis_index("grp")
    me = {"x": fsdp // RING, "y": fsdp % RING, "z": grp // 2}
    core = grp % 2

    def dev(x, y, z, c):
        return (x * RING + y, z * 2 + c)

    def near(axis, step):
        at = dict(me)
        at[axis] = (at[axis] + step) % RING
        return dev(at["x"], at["y"], at["z"], core)

    partner = dev(me["x"], me["y"], me["z"], 1 - core)

    bar = pltpu.get_barrier_semaphore()
    last_core = me["x"] // 2
    self_in = last_core == core
    own_k = (me["x"] % 2) * RING + me["y"]

    def last_dev(k):
        return dev(2 * core + k // RING, k % RING, me["z"], last_core)

    def is_self(k):
        return jnp.logical_and(self_in, own_k == k)

    for axis in ("x", "y", "z"):
        for step in FAR:
            pl.semaphore_signal(bar, inc=1, device_id=near(axis, step), device_id_type=MESH)
    pl.semaphore_signal(bar, inc=1, device_id=partner, device_id_type=MESH)
    mine = pl.ds(pl.multiple_of(core * HALF, BLK), HALF)
    other = pl.ds(pl.multiple_of((1 - core) * HALF, BLK), HALF)
    own_rows = pl.ds(pl.multiple_of(core * OWN, OWN), OWN)
    own_tokens = pl.ds(2 * core, 2)

    def slab(z):
        return pl.ds(pl.multiple_of(z * 2 * OWN, 2 * OWN), 2 * OWN)

    local = [
        pltpu.make_async_copy(*pair, loc.at[i])
        for i, pair in enumerate((
            (grad_ref, grad),
            (count_ref, count),
            (hid_ref, hb.at[core]),
            (old_ref, old_v),
            (drop_ref, drop),
            (grow_ref, grow),
            (w_ref.at[:, mine], w.at[own_rows, :]),
            (inp_ref.at[:, :, :, slab(me["z"])], xin.at[me["z"], own_tokens]),
        ))
    ]
    for c in local:
        c.start()

    def remote(src, dst, sends, recvs, i, to):
        return pltpu.make_async_remote_copy(
            src_ref=src, dst_ref=dst, send_sem=sends.at[i], recv_sem=recvs.at[i],
            device_id=to, device_id_type=MESH,
        )

    local[0].wait()
    local[1].wait()
    rows = lax.broadcasted_iota(jnp.int32, grad.shape, 0)
    gm[...] = jnp.where(rows < count[0], grad[...].astype(F32), 0.0).astype(BF)
    gp[core] = gm[:, mine]
    pl.semaphore_wait(bar, 10)

    swap = [
        remote(gm.at[:, other], gp.at[core], e_send, e_recv, 0, partner),
        remote(hid_ref, hb.at[core], e_send, e_recv, 1, partner),
        remote(m.at[core], m.at[core], e_send, e_recv, 2, partner),
        remote(w_ref.at[:, other], w.at[own_rows, :], e_send, e_recv, 3, partner),
        remote(h.at[core], h.at[core], e_send, e_recv, 4, partner),
        remote(xin.at[:, own_tokens], xin.at[:, own_tokens], e_send, e_recv, 5, partner),
    ]
    swap[0].start()
    swap[1].start()
    swap[3].start()

    inp = [
        remote(
            inp_ref.at[:, :, :, slab((me["z"] + d) % RING)], xin.at[me["z"], own_tokens],
            a_send, a_recv, i, near("z", d),
        )
        for i, d in enumerate(FAR)
    ]
    hid = []
    for u in range(2):
        for q, axis in enumerate(TURNS[u]):
            src = (t0, t1, t2)[q].at[u]
            dst = (t1.at[u], t2.at[u], h.at[core, u])[q]

            def ends_of(d):
                v = (me[axis] + d) % RING
                return src.at[pick(GDIMS, {axis: v})], dst.at[pick(GDIMS, {axis: me[axis]})]

            n = u * 3 + q
            stay = pltpu.make_async_copy(*ends_of(0), loc.at[8 + n])
            go = [
                remote(*ends_of(d), a_send, a_recv, 3 + n * 3 + i, near(axis, d))
                for i, d in enumerate(FAR)
            ]
            hid.append((stay, go))

    def hid_start(q):
        for u in range(2):
            for c in (*hid[u * 3 + q][1], hid[u * 3 + q][0]):
                c.start()

    def hid_wait(q):
        for u in range(2):
            hid[u * 3 + q][0].wait()
            for c in hid[u * 3 + q][1]:
                c.wait_recv()

    swap[0].wait_recv()
    g[me["x"], me["y"], me["z"]] = jnp.concatenate([gp[0], gp[1]], axis=0)

    sends = []

    def gather_copy(p, q, cols, at, to):
        fixed = {d: me[d] for d in GATHER[p][q:]}
        fixed[GATHER[p][q]] = at
        ref = g.at[(*pick(GDIMS, fixed), slice(None), cols)]
        sends.append(remote(ref, ref, g_send, g_recv, len(sends), to))
        return sends[-1]

    def gather_direct(p, q, off, width, half):
        axis = GATHER[p][q]
        cols = pl.ds(off, width)
        return [gather_copy(p, q, cols, me[axis], near(axis, d)) for d in FAR]

    def gather_ring(p, q, off, width, half):
        axis = GATHER[p][q]
        cols, lo, hi = pl.ds(off, width), pl.ds(off, half), pl.ds(off + half, width - half)
        return [
            gather_copy(p, q, cols, me[axis], near(axis, 1)),
            gather_copy(p, q, cols, me[axis], near(axis, 3)),
            gather_copy(p, q, lo, (me[axis] + 3) % RING, near(axis, 1)),
            gather_copy(p, q, hi, (me[axis] + 1) % RING, near(axis, 3)),
        ]

    g0 = [[gather_direct(p, 0, *PARTS[p][k]) for p in range(3)] for k in range(GROUPS)]
    g1 = [[gather_direct(p, 1, *PARTS[p][k]) for p in range(3)] for k in range(GROUPS)]
    g2 = [[gather_ring(p, 2, *PARTS[p][k]) for p in range(3)] for k in range(GROUPS)]

    def start(copies):
        for c in copies:
            c.start()

    def arrive(copies):
        for c in copies:
            c.wait_recv()

    def grad_chunk(p, k, step):
        axis = GATHER[p][2]
        at = (me[axis] + step) % RING
        lhs = ht[p, at]
        off, width, _ = PARTS[p][k]
        cols = pl.ds(off, width)
        rhs = g[(*pick(GDIMS, {axis: at}), slice(None), cols)].reshape(256, width)
        part = jnp.dot(lhs, rhs, preferred_element_type=F32)
        if step == 0:
            acc[:, cols] = part
        else:
            acc[:, cols] += part

    for k in range(GROUPS):
        for p in range(3):
            start(g0[k][p])

    for c in local[3:6]:
        c.wait()
    old = old_v[...]
    ids = lax.broadcasted_iota(jnp.int32, old.shape, 0) * old.shape[1] + lax.broadcasted_iota(
        jnp.int32, old.shape, 1
    )
    new = old
    for i in range(drop.shape[1]):
        new = jnp.where(ids == drop[0, i], 0, new)
    for i in range(grow.shape[1]):
        new = jnp.where(ids == grow[0, i], 1, new)
    mask_ref[...] = new
    m[core] = jnp.zeros((8, BLK), F32)
    m[core, 0:2, 0 : old.shape[1]] = new.astype(F32)
    m[core, 2:4, 0 : old.shape[1]] = (new * old).astype(F32)
    swap[2].start()

    local[2].wait()
    swap[1].wait_recv()

    def sort_hidden(j, carry):
        for u in range(2):
            cols = pl.ds(pl.multiple_of(j * 2 * OWN + core * OWN + u * BLK, BLK), BLK)
            both = jnp.concatenate([hb[0, :, cols], hb[1, :, cols]], axis=0)
            t0[u, j // 16, j // 4 % 4, j % 4] = both
        return carry

    lax.fori_loop(0, 64, sort_hidden, 0)
    hid_start(0)
    start(inp)

    def spread(t, carry):
        o = pl.multiple_of(t * BLK, BLK)
        block = lax.broadcasted_iota(jnp.int32, (BLK, BLK), 0) == core * (HALF // BLK) + t
        for i in range(2):
            expand[i, :, pl.ds(o, BLK)] = jnp.dot(
                m[i], block.astype(F32), preferred_element_type=F32
            )
        return carry

    def turn(i, carry):
        for p in range(3):
            sel = pick(GDIMS, {GATHER[p][2]: i})
            for n in range(4):
                part = h[(n // 2, n % 2, *sel)].reshape(256, BLK)
                ht[p, i, pl.ds(n * BLK, BLK), :] = part.T
        return carry

    for k in range(GROUPS):
        for p in range(3):
            arrive(g0[k][p])
            start(g1[k][p])
    hid_wait(0)
    hid_start(1)
    swap[2].wait_recv()
    lax.fori_loop(0, HALF // BLK, spread, 0)
    for p in range(3):
        arrive(g1[0][p])
        start(g2[0][p][:2])
    hid_wait(1)
    hid_start(2)
    for p in range(3):
        arrive(g1[1][p])
    local[7].wait()
    arrive(inp)
    swap[5].start()
    for p in range(3):
        arrive(g2[0][p][:2])
        start(g2[0][p][2:])
        start(g2[1][p][:2])
    hid_wait(2)
    swap[4].start()
    swap[4].wait_recv()
    lax.fori_loop(0, RING, turn, 0)
    for k in range(GROUPS):
        for p in range(3):
            grad_chunk(p, k, 0)
    local[6].wait()
    swap[3].wait_recv()
    swap[5].wait_recv()

    posts = []

    def scatter_copy(p, q, v, cols, into, to):
        fixed = {d: me[d] for d in SCATTER[p][:q]}
        fixed[SCATTER[p][q]] = v
        src = s.at[(*pick(SDIMS, fixed), slice(None), cols)]
        dst = into.at[(*([slice(None)] * (3 - q)), cols)]
        posts.append(remote(src, dst, s_send, s_recv, len(posts), to))
        return posts[-1]

    def scatter_ring(p, off, width, half):
        axis = SCATTER[p][0]
        lo, hi = pl.ds(off, half), pl.ds(off + half, width - half)
        out = []
        for step, cols in ((1, lo), (3, hi)):
            out.append(scatter_copy(p, 0, (me[axis] + 2) % RING, cols, ra1, near(axis, step)))
        for i, (step, cols) in enumerate(((1, hi), (3, lo), (1, lo), (3, hi))):
            v = (me[axis] + step) % RING
            out.append(scatter_copy(p, 0, v, cols, rb1.at[i % 2], near(axis, step)))
        return out

    def scatter_direct(p, q, off, width, half):
        axis = SCATTER[p][q]
        into = (rb2, rb3)[q - 1]
        return [
            scatter_copy(p, q, (me[axis] + d) % RING, pl.ds(off, width), into.at[i], near(axis, d))
            for i, d in enumerate(FAR)
        ]

    s0 = [[scatter_ring(p, *PARTS[p][k]) for p in range(3)] for k in range(GROUPS)]
    s1 = [[scatter_direct(p, 1, *PARTS[p][k]) for p in range(3)] for k in range(GROUPS)]
    s2 = [[scatter_direct(p, 2, *PARTS[p][k]) for p in range(3)] for k in range(GROUPS)]

    def out_chunk(p, k, step):
        axis = SCATTER[p][0]
        sel = pick(SDIMS, {axis: (me[axis] + step) % RING})
        off, width, _ = PARTS[p][k]
        cols = pl.ds(off, width)
        part = jnp.dot(xin[sel].reshape(256, 2 * OWN), w[:, cols], preferred_element_type=F32)
        s[(*sel, slice(None), cols)] = part.astype(BF).reshape(RING, RING, ROWS, width)

    def update(p, k):
        off, width, _ = PARTS[p][k]
        cols = pl.ds(off, width)
        for r in range(4):
            side, row = r // 2, r % 2
            keep = expand[side, row : row + 1, cols]
            both = expand[side, row + 2 : row + 3, cols]
            span = pl.ds(r * BLK, BLK)
            w[span, cols] = (both * w[span, cols].astype(F32) - keep * acc[span, cols]).astype(BF)

    def add_into(p, q, v, cols, froms):
        fixed = {d: me[d] for d in SCATTER[p][:q]}
        fixed[SCATTER[p][q]] = v
        free = [d for d in SDIMS if d not in fixed]

        def one(lead):
            idx = dict(fixed)
            if free:
                idx[free[0]] = lead
            at = (*pick(SDIMS, idx), slice(None), cols)
            there = ((lead,) if free else ()) + (slice(None),) * (len(free) - 1 if free else 0)
            total = s[at].astype(F32)
            for ref, pre in froms:
                total = total + ref[(*pre, *there, slice(None), cols)].astype(F32)
            return at, total

        if not free:
            return one(None)[1]

        def step(i, carry):
            at, total = one(i)
            s[at] = total.astype(BF)
            return carry

        lax.fori_loop(0, RING, step, 0)
        return None

    def finish(k):
        for p in range(3):
            arrive(g2[k][p][2:])
            grad_chunk(p, k, 2)
            update(p, k)
            out_chunk(p, k, 2)
            start(s0[k][p][:2])

    def sides(k):
        for p in range(3):
            out_chunk(p, k, 1)
            s0[k][p][2].start()
            out_chunk(p, k, 3)
            s0[k][p][3].start()

    def relay(k):
        for p in range(3):
            off, width, half = PARTS[p][k]
            for i, cols in enumerate((pl.ds(off, half), pl.ds(off + half, width - half))):
                s0[k][p][i].wait_recv()
                add_into(p, 0, (me[SCATTER[p][0]] + (1, 3)[i]) % RING, cols, [(ra1, ())])
                s0[k][p][4 + i].start()

    def settle(k):
        for p in range(3):
            off, width, _ = PARTS[p][k]
            arrive(s0[k][p][2:])
            add_into(p, 0, me[SCATTER[p][0]], pl.ds(off, width), [(rb1, (0,)), (rb1, (1,))])
            start(s1[k][p])

    for p in range(3):
        grad_chunk(p, 0, 1)
        grad_chunk(p, 0, 3)
    finish(0)
    for p in range(3):
        arrive(g2[1][p][:2])
        start(g2[1][p][2:])
    sides(0)
    for p in range(3):
        grad_chunk(p, 1, 1)
        grad_chunk(p, 1, 3)
    relay(0)
    finish(1)
    sides(1)
    for k in range(GROUPS):
        for p in range(3):
            out_chunk(p, k, 0)
    relay(1)
    settle(0)
    settle(1)
    for k in range(GROUPS):
        for p in range(3):
            off, width, _ = PARTS[p][k]
            arrive(s1[k][p])
            add_into(p, 1, me[SCATTER[p][1]], pl.ds(off, width), [(rb2, (i,)) for i in range(3)])
            start(s2[k][p])
    slot = fsdp % 8
    ends = []

    def deliver(k):
        base, shift = CHUNK * k // BLK * BLK, CHUNK * k % BLK
        piece = fin[:, pl.ds(base, PAD + BLK)]
        if shift:
            piece = pltpu.roll(piece, PAD + BLK - shift, 1)
        stage[k] = piece[:, :PAD].astype(BF)
        away = pltpu.make_async_remote_copy(
            src_ref=stage.at[k], dst_ref=land.at[slot], send_sem=f_send.at[k],
            recv_sem=f_recv.at[slot], device_id=last_dev(k), device_id_type=MESH,
        )

        @pl.when(jnp.logical_not(is_self(k)))
        def _():
            away.start()

        @pl.when(is_self(k))
        def _():
            pltpu.make_async_copy(stage.at[k], land.at[slot], f_recv.at[slot]).start()

        ends.append(away)

    fin[:, pl.ds(HALF, BLK)] = jnp.zeros((ROWS, BLK), F32)
    for k in range(GROUPS):
        for p in range(3):
            off, width, _ = PARTS[p][k]
            arrive(s2[k][p])
            total = add_into(p, 2, me[SCATTER[p][2]], pl.ds(off, width), [(rb3, (i,)) for i in range(3)])
            fin[:, pl.ds(off, width)] = total
        for n in range(4 * k, 4 * k + 4):
            deliver(n)
    for k in range(8):
        pltpu.make_async_copy(stage.at[k], land.at[k], f_recv.at[k]).wait()
        out_ref[pl.ds(k * ROWS, ROWS), :] = land[k][:, :CHUNK]

    for k in range(8):
        @pl.when(jnp.logical_not(is_self(k)))
        def _():
            ends[k].wait_send()
    for c in swap:
        c.wait_send()
    for c in (*sends, *posts):
        c.wait_send()
    for c in (*inp, *(c for pair in hid for c in pair[1])):
        c.wait_send()


def shards(hidden, grad_out, token_counts, weight, old_mask, drop_list, grow_list, inputs):
    inp = inputs.reshape(2, RING, ROWS, 2048)
    vmem = pl.BlockSpec(memory_space=pltpu.VMEM)
    hbm = pl.BlockSpec(memory_space=pl.ANY)
    dma = pltpu.SemaphoreType.DMA
    cube = (RING, RING, RING, ROWS)
    out, mask = pl.pallas_call(
        kernel,
        out_shape=(
            jax.ShapeDtypeStruct((128, CHUNK), BF),
            jax.ShapeDtypeStruct(old_mask.shape, jnp.int32),
        ),
        in_specs=[hbm] * 8,
        out_specs=(vmem, vmem),
        scratch_shapes=[
            pltpu.SMEM((1,), jnp.int32),
            pltpu.SMEM(drop_list.shape, jnp.int32),
            pltpu.SMEM(grow_list.shape, jnp.int32),
            pltpu.VMEM(old_mask.shape, jnp.int32),
            pltpu.VMEM((8, 2 * HALF), BF),
            pltpu.VMEM((8, 2 * HALF), BF),
            pltpu.VMEM((2, 8, HALF), BF),
            pltpu.VMEM((*cube, HALF), BF),
            pltpu.VMEM((2, 8, 64 * 2 * OWN), BF),
            pltpu.VMEM((2, *cube, BLK), BF),
            pltpu.VMEM((2, *cube, BLK), BF),
            pltpu.VMEM((2, *cube, BLK), BF),
            pltpu.VMEM((2, 2, *cube, BLK), BF),
            pltpu.VMEM((3, RING, 2 * OWN, 256), BF),
            pltpu.VMEM((2 * OWN, HALF), F32),
            pltpu.VMEM((2 * OWN, HALF), BF),
            pltpu.VMEM((*cube, 2 * OWN), BF),
            pltpu.VMEM((*cube, HALF), BF),
            pltpu.VMEM((2, 8, BLK), F32),
            pltpu.VMEM((2, 8, HALF), F32),
            pltpu.VMEM((RING, RING, ROWS, HALF), BF),
            pltpu.VMEM((2, RING, RING, ROWS, HALF), BF),
            pltpu.VMEM((3, RING, ROWS, HALF), BF),
            pltpu.VMEM((3, ROWS, HALF), BF),
            pltpu.VMEM((ROWS, HALF + BLK), F32),
            pltpu.VMEM((8, ROWS, PAD), BF),
            pltpu.VMEM((8, ROWS, PAD), BF),
            dma((60,)), dma((60,)), dma((72,)), dma((72,)), dma((6,)), dma((6,)),
            dma((8,)), dma((8,)), dma((21,)), dma((21,)), dma((14,)),
        ],
        compiler_params=pltpu.CompilerParams(
            collective_id=0, has_side_effects=True, vmem_limit_bytes=60 * 2**20
        ),
        cost_estimate=pl.CostEstimate(flops=8 * 10**9, bytes_accessed=10**7, transcendentals=0),
    )(token_counts, drop_list, grow_list, old_mask, grad_out, hidden, inp, weight)
    return (out, mask)


def solution(mesh):
    split = P(("fsdp", "grp"), None)
    return jax.shard_map(
        shards,
        mesh=mesh,
        in_specs=(split, split, P(("fsdp", "grp")), split, split, split, split, P("grp", "fsdp")),
        out_specs=(P("grp", "fsdp"), split),
        check_vma=False,
    )
```

```python
import jax
import jax.numpy as jnp
from jax import lax
from jax.experimental import pallas as pl
from jax.experimental.pallas import tpu as pltpu
from jax.sharding import PartitionSpec as P

MESH = pl.DeviceIdType.MESH
BF = jnp.bfloat16
F32 = jnp.float32

RING = 4
ROWS = 16
BLK = 128
HALF = 3712
OWN = 256
CHUNK = 464
PAD = 512

PARTS = (
    ((0, 640, 384), (2176, 512, 256)),
    ((640, 768, 384), (2688, 512, 256)),
    ((1408, 768, 384), (3200, 512, 256)),
)
GROUPS = 2
FAR = (1, 3, 2)
TURNS = (("x", "y", "z"), ("y", "z", "x"))
GATHER = (("x", "y", "z"), ("y", "z", "x"), ("z", "x", "y"))
SCATTER = (("x", "y", "z"), ("y", "z", "x"), ("z", "x", "y"))
GDIMS = ("x", "y", "z")
SDIMS = ("z", "x", "y")


def pick(dims, fixed):
    return tuple(fixed[d] if d in fixed else slice(None) for d in dims)


def kernel(
    count_ref, drop_ref, grow_ref, old_ref, grad_ref, hid_ref, inp_ref, w_ref,
    out_ref, mask_ref,
    count, drop, grow, old_v, grad, gm, gp, g, hb, t0, t1, t2, h, ht, acc, w, xin, s, m, expand, ra1, rb1, rb2, rb3, fin, stage, land,
    g_send, g_recv, s_send, s_recv, e_send, e_recv, f_send, f_recv, a_send, a_recv, loc,
):
    fsdp = lax.axis_index("fsdp")
    grp = lax.axis_index("grp")
    me = {"x": fsdp // RING, "y": fsdp % RING, "z": grp // 2}
    core = grp % 2

    def dev(x, y, z, c):
        return (x * RING + y, z * 2 + c)

    def near(axis, step):
        at = dict(me)
        at[axis] = (at[axis] + step) % RING
        return dev(at["x"], at["y"], at["z"], core)

    partner = dev(me["x"], me["y"], me["z"], 1 - core)

    bar = pltpu.get_barrier_semaphore()
    last_core = me["x"] // 2
    self_in = last_core == core
    own_k = (me["x"] % 2) * RING + me["y"]

    def last_dev(k):
        return dev(2 * core + k // RING, k % RING, me["z"], last_core)

    def is_self(k):
        return jnp.logical_and(self_in, own_k == k)

    for axis in ("x", "y", "z"):
        for step in FAR:
            pl.semaphore_signal(bar, inc=1, device_id=near(axis, step), device_id_type=MESH)
    pl.semaphore_signal(bar, inc=1, device_id=partner, device_id_type=MESH)
    mine = pl.ds(pl.multiple_of(core * HALF, BLK), HALF)
    other = pl.ds(pl.multiple_of((1 - core) * HALF, BLK), HALF)
    own_rows = pl.ds(pl.multiple_of(core * OWN, OWN), OWN)
    own_tokens = pl.ds(2 * core, 2)

    def slab(z):
        return pl.ds(pl.multiple_of(z * 2 * OWN, 2 * OWN), 2 * OWN)

    local = [
        pltpu.make_async_copy(*pair, loc.at[i])
        for i, pair in enumerate((
            (grad_ref, grad),
            (count_ref, count),
            (hid_ref, hb.at[core]),
            (old_ref, old_v),
            (drop_ref, drop),
            (grow_ref, grow),
            (w_ref.at[:, mine], w.at[own_rows, :]),
            (inp_ref.at[:, :, :, slab(me["z"])], xin.at[me["z"], own_tokens]),
        ))
    ]
    for c in local:
        c.start()

    def remote(src, dst, send, recv, to):
        return pltpu.make_async_remote_copy(
            src_ref=src, dst_ref=dst, send_sem=send, recv_sem=recv,
            device_id=to, device_id_type=MESH,
        )

    def wait_for(like, sem):
        pltpu.make_async_copy(like, like, sem).wait()

    local[0].wait()
    local[1].wait()
    rows = lax.broadcasted_iota(jnp.int32, grad.shape, 0)
    gm[...] = jnp.where(rows < count[0], grad[...].astype(F32), 0.0).astype(BF)
    gp[core] = gm[:, mine]
    pl.semaphore_wait(bar, 10)

    swap = [
        remote(gm.at[:, other], gp.at[core], e_send.at[0], e_recv.at[0], partner),
        remote(hid_ref, hb.at[core], e_send.at[1], e_recv.at[1], partner),
        remote(m.at[core], m.at[core], e_send.at[2], e_recv.at[2], partner),
        remote(w_ref.at[:, other], w.at[own_rows, :], e_send.at[3], e_recv.at[3], partner),
        remote(h.at[core], h.at[core], e_send.at[4], e_recv.at[4], partner),
        remote(xin.at[:, own_tokens], xin.at[:, own_tokens], e_send.at[5], e_recv.at[5], partner),
    ]
    swap[0].start()
    swap[1].start()
    swap[3].start()

    inp = [
        remote(
            inp_ref.at[:, :, :, slab((me["z"] + d) % RING)], xin.at[me["z"], own_tokens],
            a_send.at[3], a_recv.at[3], near("z", d),
        )
        for d in FAR
    ]
    hid = []
    for u in range(2):
        for q, axis in enumerate(TURNS[u]):
            src = (t0, t1, t2)[q].at[u]
            dst = (t1.at[u], t2.at[u], h.at[core, u])[q]

            def ends_of(d):
                v = (me[axis] + d) % RING
                return src.at[pick(GDIMS, {axis: v})], dst.at[pick(GDIMS, {axis: me[axis]})]

            stay = pltpu.make_async_copy(*ends_of(0), loc.at[8 + u * 3 + q])
            go = [remote(*ends_of(d), a_send.at[q], a_recv.at[q], near(axis, d)) for d in FAR]
            hid.append((stay, go))

    def hid_start(q):
        for u in range(2):
            for c in (*hid[u * 3 + q][1], hid[u * 3 + q][0]):
                c.start()

    def hid_wait(q):
        for u in range(2):
            hid[u * 3 + q][0].wait()
        wait_for(t0.at[:, 0:3], a_recv.at[q])

    swap[0].wait_recv()
    g[me["x"], me["y"], me["z"]] = jnp.concatenate([gp[0], gp[1]], axis=0)

    def gather_copy(p, q, cols, at, to, send, recv):
        fixed = {d: me[d] for d in GATHER[p][q:]}
        fixed[GATHER[p][q]] = at
        ref = g.at[(*pick(GDIMS, fixed), slice(None), cols)]
        return remote(ref, ref, g_send.at[send], g_recv.at[recv], to)

    def gather_direct(k, p, q):
        off, width, _ = PARTS[p][k]
        axis = GATHER[p][q]
        cols, n = pl.ds(off, width), q * 6 + k * 3 + p
        return [gather_copy(p, q, cols, me[axis], near(axis, d), q, n) for d in FAR]

    def gather_ring(k, p):
        off, width, half = PARTS[p][k]
        axis = GATHER[p][2]
        cols, lo, hi = pl.ds(off, width), pl.ds(off, half), pl.ds(off + half, width - half)
        n = 12 + k * 3 + p
        return [
            gather_copy(p, 2, cols, me[axis], near(axis, 1), 2, n),
            gather_copy(p, 2, cols, me[axis], near(axis, 3), 2, n),
            gather_copy(p, 2, lo, (me[axis] + 3) % RING, near(axis, 1), 3, n + 6),
            gather_copy(p, 2, hi, (me[axis] + 1) % RING, near(axis, 3), 3, n + 6),
        ]

    g0 = [[gather_direct(k, p, 0) for p in range(3)] for k in range(GROUPS)]
    g1 = [[gather_direct(k, p, 1) for p in range(3)] for k in range(GROUPS)]
    g2 = [[gather_ring(k, p) for p in range(3)] for k in range(GROUPS)]

    def gathered(k, p, q):
        off, width, _ = PARTS[p][k]
        cols = pl.ds(off, width)
        like = (
            rb3.at[:, :, cols], rb2.at[:, :, :, cols], rb1.at[:, :, :, :, cols], ra1.at[:, :, :, cols]
        )[q]
        wait_for(like, g_recv.at[q * 6 + k * 3 + p])

    def start(copies):
        for c in copies:
            c.start()

    def grad_chunk(p, k, step):
        axis = GATHER[p][2]
        at = (me[axis] + step) % RING
        lhs = ht[p, at]
        off, width, _ = PARTS[p][k]
        cols = pl.ds(off, width)
        rhs = g[(*pick(GDIMS, {axis: at}), slice(None), cols)].reshape(256, width)
        part = jnp.dot(lhs, rhs, preferred_element_type=F32)
        if step == 0:
            acc[:, cols] = part
        else:
            acc[:, cols] += part

    for k in range(GROUPS):
        for p in range(3):
            start(g0[k][p])

    for c in local[3:6]:
        c.wait()
    old = old_v[...]
    ids = lax.broadcasted_iota(jnp.int32, old.shape, 0) * old.shape[1] + lax.broadcasted_iota(
        jnp.int32, old.shape, 1
    )
    new = old
    for i in range(drop.shape[1]):
        new = jnp.where(ids == drop[0, i], 0, new)
    for i in range(grow.shape[1]):
        new = jnp.where(ids == grow[0, i], 1, new)
    mask_ref[...] = new
    m[core] = jnp.zeros((8, BLK), F32)
    m[core, 0:2, 0 : old.shape[1]] = new.astype(F32)
    m[core, 2:4, 0 : old.shape[1]] = (new * old).astype(F32)
    swap[2].start()

    local[2].wait()
    swap[1].wait_recv()

    def sort_hidden(j, carry):
        for u in range(2):
            cols = pl.ds(pl.multiple_of(j * 2 * OWN + core * OWN + u * BLK, BLK), BLK)
            both = jnp.concatenate([hb[0, :, cols], hb[1, :, cols]], axis=0)
            t0[u, j // 16, j // 4 % 4, j % 4] = both
        return carry

    lax.fori_loop(0, 64, sort_hidden, 0)
    hid_start(0)
    start(inp)

    def spread(t, carry):
        o = pl.multiple_of(t * BLK, BLK)
        block = lax.broadcasted_iota(jnp.int32, (BLK, BLK), 0) == core * (HALF // BLK) + t
        for i in range(2):
            expand[i, :, pl.ds(o, BLK)] = jnp.dot(
                m[i], block.astype(F32), preferred_element_type=F32
            )
        return carry

    def turn(i, carry):
        for p in range(3):
            sel = pick(GDIMS, {GATHER[p][2]: i})
            for n in range(4):
                part = h[(n // 2, n % 2, *sel)].reshape(256, BLK)
                ht[p, i, pl.ds(n * BLK, BLK), :] = part.T
        return carry

    for k in range(GROUPS):
        for p in range(3):
            gathered(k, p, 0)
            start(g1[k][p])
    hid_wait(0)
    hid_start(1)
    swap[2].wait_recv()
    lax.fori_loop(0, HALF // BLK, spread, 0)
    for p in range(3):
        gathered(0, p, 1)
        start(g2[0][p][:2])
    hid_wait(1)
    hid_start(2)
    for p in range(3):
        gathered(1, p, 1)
    local[7].wait()
    wait_for(xin.at[0:3, own_tokens], a_recv.at[3])
    swap[5].start()
    for p in range(3):
        gathered(0, p, 2)
        start(g2[0][p][2:])
        start(g2[1][p][:2])
    hid_wait(2)
    swap[4].start()
    swap[4].wait_recv()
    lax.fori_loop(0, RING, turn, 0)
    for k in range(GROUPS):
        for p in range(3):
            grad_chunk(p, k, 0)
    local[6].wait()
    swap[3].wait_recv()
    swap[5].wait_recv()

    def scatter_copy(p, q, v, cols, into, to, send, recv):
        fixed = {d: me[d] for d in SCATTER[p][:q]}
        fixed[SCATTER[p][q]] = v
        src = s.at[(*pick(SDIMS, fixed), slice(None), cols)]
        dst = into.at[(*([slice(None)] * (3 - q)), cols)]
        return remote(src, dst, s_send.at[send], s_recv.at[recv], to)

    def scatter_ring(k, p):
        off, width, half = PARTS[p][k]
        axis = SCATTER[p][0]
        lo, hi, n = pl.ds(off, half), pl.ds(off + half, width - half), k * 3 + p
        out = []
        for step, cols in ((1, lo), (3, hi)):
            v = (me[axis] + 2) % RING
            out.append(scatter_copy(p, 0, v, cols, ra1, near(axis, step), 0, n))
        for i, (step, cols) in enumerate(((1, hi), (3, lo), (1, lo), (3, hi))):
            v = (me[axis] + step) % RING
            out.append(scatter_copy(p, 0, v, cols, rb1.at[i % 2], near(axis, step), 1, 6 + n))
        return out

    def scatter_direct(k, p, q):
        off, width, _ = PARTS[p][k]
        axis = SCATTER[p][q]
        into, cols, n = (rb2, rb3)[q - 1], pl.ds(off, width), 6 + q * 6 + k * 3 + p
        return [
            scatter_copy(p, q, (me[axis] + d) % RING, cols, into.at[i], near(axis, d), 1 + q, n)
            for i, d in enumerate(FAR)
        ]

    s0 = [[scatter_ring(k, p) for p in range(3)] for k in range(GROUPS)]
    s1 = [[scatter_direct(k, p, 1) for p in range(3)] for k in range(GROUPS)]
    s2 = [[scatter_direct(k, p, 2) for p in range(3)] for k in range(GROUPS)]

    def scattered(k, p, q):
        off, width, _ = PARTS[p][k]
        cols = pl.ds(off, width)
        like = (
            ra1.at[:, :, :, cols], rb1.at[:, :, :, :, cols], rb2.at[:, :, :, cols], rb3.at[:, :, cols]
        )[q]
        wait_for(like, s_recv.at[q * 6 + k * 3 + p])

    def out_chunk(p, k, step):
        axis = SCATTER[p][0]
        sel = pick(SDIMS, {axis: (me[axis] + step) % RING})
        off, width, _ = PARTS[p][k]
        cols = pl.ds(off, width)
        part = jnp.dot(xin[sel].reshape(256, 2 * OWN), w[:, cols], preferred_element_type=F32)
        s[(*sel, slice(None), cols)] = part.astype(BF).reshape(RING, RING, ROWS, width)

    def update(p, k):
        off, width, _ = PARTS[p][k]
        cols = pl.ds(off, width)
        for r in range(4):
            side, row = r // 2, r % 2
            keep = expand[side, row : row + 1, cols]
            both = expand[side, row + 2 : row + 3, cols]
            span = pl.ds(r * BLK, BLK)
            w[span, cols] = (both * w[span, cols].astype(F32) - keep * acc[span, cols]).astype(BF)

    def add_into(p, q, v, cols, froms):
        fixed = {d: me[d] for d in SCATTER[p][:q]}
        fixed[SCATTER[p][q]] = v
        free = [d for d in SDIMS if d not in fixed]

        def one(lead):
            idx = dict(fixed)
            if free:
                idx[free[0]] = lead
            at = (*pick(SDIMS, idx), slice(None), cols)
            there = ((lead,) if free else ()) + (slice(None),) * (len(free) - 1 if free else 0)
            total = s[at].astype(F32)
            for ref, pre in froms:
                total = total + ref[(*pre, *there, slice(None), cols)].astype(F32)
            return at, total

        if not free:
            return one(None)[1]

        def step(i, carry):
            at, total = one(i)
            s[at] = total.astype(BF)
            return carry

        lax.fori_loop(0, RING, step, 0)
        return None

    def finish(k):
        for p in range(3):
            gathered(k, p, 3)
            grad_chunk(p, k, 2)
            update(p, k)
            out_chunk(p, k, 2)
            start(s0[k][p][:2])

    def sides(k):
        for p in range(3):
            out_chunk(p, k, 1)
            s0[k][p][2].start()
            out_chunk(p, k, 3)
            s0[k][p][3].start()

    def relay(k):
        for p in range(3):
            off, width, half = PARTS[p][k]
            scattered(k, p, 0)
            for i, cols in enumerate((pl.ds(off, half), pl.ds(off + half, width - half))):
                add_into(p, 0, (me[SCATTER[p][0]] + (1, 3)[i]) % RING, cols, [(ra1, ())])
                s0[k][p][4 + i].start()

    def settle(k):
        for p in range(3):
            off, width, _ = PARTS[p][k]
            scattered(k, p, 1)
            add_into(p, 0, me[SCATTER[p][0]], pl.ds(off, width), [(rb1, (0,)), (rb1, (1,))])
            start(s1[k][p])

    for p in range(3):
        grad_chunk(p, 0, 1)
        grad_chunk(p, 0, 3)
    finish(0)
    for p in range(3):
        gathered(1, p, 2)
        start(g2[1][p][2:])
    sides(0)
    for p in range(3):
        grad_chunk(p, 1, 1)
        grad_chunk(p, 1, 3)
    relay(0)
    finish(1)
    sides(1)
    for k in range(GROUPS):
        for p in range(3):
            out_chunk(p, k, 0)
    relay(1)
    settle(0)
    settle(1)
    for k in range(GROUPS):
        for p in range(3):
            off, width, _ = PARTS[p][k]
            scattered(k, p, 2)
            add_into(p, 1, me[SCATTER[p][1]], pl.ds(off, width), [(rb2, (i,)) for i in range(3)])
            start(s2[k][p])
    slot = fsdp % 8
    ends = []

    def deliver(k):
        base, shift = CHUNK * k // BLK * BLK, CHUNK * k % BLK
        piece = fin[:, pl.ds(base, PAD + BLK)]
        if shift:
            piece = pltpu.roll(piece, PAD + BLK - shift, 1)
        stage[k] = piece[:, :PAD].astype(BF)
        away = pltpu.make_async_remote_copy(
            src_ref=stage.at[k], dst_ref=land.at[slot], send_sem=f_send.at[k],
            recv_sem=f_recv.at[slot], device_id=last_dev(k), device_id_type=MESH,
        )

        @pl.when(jnp.logical_not(is_self(k)))
        def _():
            away.start()

        @pl.when(is_self(k))
        def _():
            pltpu.make_async_copy(stage.at[k], land.at[slot], f_recv.at[slot]).start()

        ends.append(away)

    fin[:, pl.ds(HALF, BLK)] = jnp.zeros((ROWS, BLK), F32)
    for k in range(GROUPS):
        for p in range(3):
            off, width, _ = PARTS[p][k]
            scattered(k, p, 3)
            total = add_into(p, 2, me[SCATTER[p][2]], pl.ds(off, width), [(rb3, (i,)) for i in range(3)])
            fin[:, pl.ds(off, width)] = total
        for n in range(4 * k, 4 * k + 4):
            deliver(n)
    for k in range(8):
        pltpu.make_async_copy(stage.at[k], land.at[k], f_recv.at[k]).wait()
        out_ref[pl.ds(k * ROWS, ROWS), :] = land[k][:, :CHUNK]

    for k in range(8):
        @pl.when(jnp.logical_not(is_self(k)))
        def _():
            ends[k].wait_send()
    for c in swap:
        c.wait_send()
    for i, like in enumerate((rb3, rb2, rb1, ra1)):
        wait_for(like, g_send.at[i])
    for i, like in enumerate((ra1, rb1, rb2, rb3)):
        wait_for(like, s_send.at[i])
    for i in range(3):
        wait_for(t0.at[:, 0:3], a_send.at[i])
    wait_for(xin.at[0:3, own_tokens], a_send.at[3])


def shards(hidden, grad_out, token_counts, weight, old_mask, drop_list, grow_list, inputs):
    inp = inputs.reshape(2, RING, ROWS, 2048)
    vmem = pl.BlockSpec(memory_space=pltpu.VMEM)
    hbm = pl.BlockSpec(memory_space=pl.ANY)
    dma = pltpu.SemaphoreType.DMA
    cube = (RING, RING, RING, ROWS)
    out, mask = pl.pallas_call(
        kernel,
        out_shape=(
            jax.ShapeDtypeStruct((128, CHUNK), BF),
            jax.ShapeDtypeStruct(old_mask.shape, jnp.int32),
        ),
        in_specs=[hbm] * 8,
        out_specs=(vmem, vmem),
        scratch_shapes=[
            pltpu.SMEM((1,), jnp.int32),
            pltpu.SMEM(drop_list.shape, jnp.int32),
            pltpu.SMEM(grow_list.shape, jnp.int32),
            pltpu.VMEM(old_mask.shape, jnp.int32),
            pltpu.VMEM((8, 2 * HALF), BF),
            pltpu.VMEM((8, 2 * HALF), BF),
            pltpu.VMEM((2, 8, HALF), BF),
            pltpu.VMEM((*cube, HALF), BF),
            pltpu.VMEM((2, 8, 64 * 2 * OWN), BF),
            pltpu.VMEM((2, *cube, BLK), BF),
            pltpu.VMEM((2, *cube, BLK), BF),
            pltpu.VMEM((2, *cube, BLK), BF),
            pltpu.VMEM((2, 2, *cube, BLK), BF),
            pltpu.VMEM((3, RING, 2 * OWN, 256), BF),
            pltpu.VMEM((2 * OWN, HALF), F32),
            pltpu.VMEM((2 * OWN, HALF), BF),
            pltpu.VMEM((*cube, 2 * OWN), BF),
            pltpu.VMEM((*cube, HALF), BF),
            pltpu.VMEM((2, 8, BLK), F32),
            pltpu.VMEM((2, 8, HALF), F32),
            pltpu.VMEM((RING, RING, ROWS, HALF), BF),
            pltpu.VMEM((2, RING, RING, ROWS, HALF), BF),
            pltpu.VMEM((3, RING, ROWS, HALF), BF),
            pltpu.VMEM((3, ROWS, HALF), BF),
            pltpu.VMEM((ROWS, HALF + BLK), F32),
            pltpu.VMEM((8, ROWS, PAD), BF),
            pltpu.VMEM((8, ROWS, PAD), BF),
            dma((4,)), dma((24,)), dma((4,)), dma((24,)), dma((6,)), dma((6,)),
            dma((8,)), dma((8,)), dma((4,)), dma((4,)), dma((14,)),
        ],
        compiler_params=pltpu.CompilerParams(
            collective_id=0, has_side_effects=True, vmem_limit_bytes=60 * 2**20
        ),
        cost_estimate=pl.CostEstimate(flops=8 * 10**9, bytes_accessed=10**7, transcendentals=0),
    )(token_counts, drop_list, grow_list, old_mask, grad_out, hidden, inp, weight)
    return (out, mask)


def solution(mesh):
    split = P(("fsdp", "grp"), None)
    return jax.shard_map(
        shards,
        mesh=mesh,
        in_specs=(split, split, P(("fsdp", "grp")), split, split, split, split, P("grp", "fsdp")),
        out_specs=(P("grp", "fsdp"), split),
        check_vma=False,
    )
```

```python
import jax
import jax.numpy as jnp
from jax import lax
from jax.experimental import pallas as pl
from jax.experimental.pallas import tpu as pltpu
from jax.sharding import PartitionSpec as P

MESH = pl.DeviceIdType.MESH
BF = jnp.bfloat16
F32 = jnp.float32

RING = 4
ROWS = 16
BLK = 128
HALF = 3712
OWN = 256
CHUNK = 464
PAD = 512

PARTS = (
    ((0, 640, 384), (2176, 512, 256)),
    ((640, 768, 384), (2688, 512, 256)),
    ((1408, 768, 384), (3200, 512, 256)),
)
GROUPS = 2
FAR = (1, 3, 2)
TURNS = (("x", "y", "z"), ("y", "z", "x"))
GATHER = (("x", "y", "z"), ("y", "z", "x"), ("z", "x", "y"))
SCATTER = (("z", "x", "y"), ("x", "y", "z"), ("y", "z", "x"))
GDIMS = ("x", "y", "z")
SDIMS = ("z", "x", "y")


def pick(dims, fixed):
    return tuple(fixed[d] if d in fixed else slice(None) for d in dims)


def kernel(
    count_ref, drop_ref, grow_ref, old_ref, grad_ref, hid_ref, inp_ref, w_ref,
    out_ref, mask_ref,
    count, drop, grow, old_v, grad, gm, gp, g, hb, t0, t1, t2, h, ht, acc, w, xin, s, m, expand, ra1, rb1, rb2, rb3, fin, stage, land,
    g_send, g_recv, s_send, s_recv, e_send, e_recv, f_send, f_recv, a_send, a_recv, loc,
):
    fsdp = lax.axis_index("fsdp")
    grp = lax.axis_index("grp")
    me = {"x": fsdp // RING, "y": fsdp % RING, "z": grp // 2}
    core = grp % 2

    def dev(x, y, z, c):
        return (x * RING + y, z * 2 + c)

    def near(axis, step):
        at = dict(me)
        at[axis] = (at[axis] + step) % RING
        return dev(at["x"], at["y"], at["z"], core)

    partner = dev(me["x"], me["y"], me["z"], 1 - core)

    bar = pltpu.get_barrier_semaphore()
    last_core = me["x"] // 2
    self_in = last_core == core
    own_k = (me["x"] % 2) * RING + me["y"]

    def last_dev(k):
        return dev(2 * core + k // RING, k % RING, me["z"], last_core)

    def is_self(k):
        return jnp.logical_and(self_in, own_k == k)

    for axis in ("x", "y", "z"):
        for step in FAR:
            pl.semaphore_signal(bar, inc=1, device_id=near(axis, step), device_id_type=MESH)
    pl.semaphore_signal(bar, inc=1, device_id=partner, device_id_type=MESH)
    mine = pl.ds(pl.multiple_of(core * HALF, BLK), HALF)
    other = pl.ds(pl.multiple_of((1 - core) * HALF, BLK), HALF)
    own_rows = pl.ds(pl.multiple_of(core * OWN, OWN), OWN)
    own_tokens = pl.ds(2 * core, 2)

    def slab(z):
        return pl.ds(pl.multiple_of(z * 2 * OWN, 2 * OWN), 2 * OWN)

    local = [
        pltpu.make_async_copy(*pair, loc.at[i])
        for i, pair in enumerate((
            (grad_ref, grad),
            (count_ref, count),
            (hid_ref, hb.at[core]),
            (old_ref, old_v),
            (drop_ref, drop),
            (grow_ref, grow),
            (w_ref.at[:, mine], w.at[own_rows, :]),
            (inp_ref.at[:, :, :, slab(me["z"])], xin.at[me["z"], own_tokens]),
        ))
    ]
    for c in local:
        c.start()

    def remote(src, dst, send, recv, to):
        return pltpu.make_async_remote_copy(
            src_ref=src, dst_ref=dst, send_sem=send, recv_sem=recv,
            device_id=to, device_id_type=MESH,
        )

    def wait_for(like, sem):
        pltpu.make_async_copy(like, like, sem).wait()

    local[0].wait()
    local[1].wait()
    rows = lax.broadcasted_iota(jnp.int32, grad.shape, 0)
    gm[...] = jnp.where(rows < count[0], grad[...].astype(F32), 0.0).astype(BF)
    gp[core] = gm[:, mine]
    pl.semaphore_wait(bar, 10)

    swap = [
        remote(gm.at[:, other], gp.at[core], e_send.at[0], e_recv.at[0], partner),
        remote(hid_ref, hb.at[core], e_send.at[1], e_recv.at[1], partner),
        remote(m.at[core], m.at[core], e_send.at[2], e_recv.at[2], partner),
        remote(w_ref.at[:, other], w.at[own_rows, :], e_send.at[3], e_recv.at[3], partner),
        remote(h.at[core], h.at[core], e_send.at[4], e_recv.at[4], partner),
        remote(xin.at[:, own_tokens], xin.at[:, own_tokens], e_send.at[5], e_recv.at[5], partner),
    ]
    swap[0].start()
    swap[1].start()
    swap[3].start()

    inp = [
        remote(
            inp_ref.at[:, :, :, slab((me["z"] + d) % RING)], xin.at[me["z"], own_tokens],
            a_send.at[3], a_recv.at[3], near("z", d),
        )
        for d in FAR
    ]
    hid = []
    for u in range(2):
        for q, axis in enumerate(TURNS[u]):
            src = (t0, t1, t2)[q].at[u]
            dst = (t1.at[u], t2.at[u], h.at[core, u])[q]

            def ends_of(d):
                v = (me[axis] + d) % RING
                return src.at[pick(GDIMS, {axis: v})], dst.at[pick(GDIMS, {axis: me[axis]})]

            stay = pltpu.make_async_copy(*ends_of(0), loc.at[8 + u * 3 + q])
            go = [remote(*ends_of(d), a_send.at[q], a_recv.at[q], near(axis, d)) for d in FAR]
            hid.append((stay, go))

    def hid_start(q):
        for u in range(2):
            for c in (*hid[u * 3 + q][1], hid[u * 3 + q][0]):
                c.start()

    def hid_wait(q):
        for u in range(2):
            hid[u * 3 + q][0].wait()
        wait_for(t0.at[:, 0:3], a_recv.at[q])

    for c in inp:
        c.start()
    swap[0].wait_recv()
    g[me["x"], me["y"], me["z"]] = jnp.concatenate([gp[0], gp[1]], axis=0)

    def gather_copy(p, q, cols, at, to, send, recv):
        fixed = {d: me[d] for d in GATHER[p][q:]}
        fixed[GATHER[p][q]] = at
        ref = g.at[(*pick(GDIMS, fixed), slice(None), cols)]
        return remote(ref, ref, g_send.at[send], g_recv.at[recv], to)

    def gather_direct(k, p, q):
        off, width, _ = PARTS[p][k]
        axis = GATHER[p][q]
        cols, n = pl.ds(off, width), q * 6 + k * 3 + p
        return [gather_copy(p, q, cols, me[axis], near(axis, d), q, n) for d in FAR]

    def gather_ring(k, p):
        off, width, half = PARTS[p][k]
        axis = GATHER[p][2]
        cols, lo, hi = pl.ds(off, width), pl.ds(off, half), pl.ds(off + half, width - half)
        n = 12 + k * 3 + p
        return [
            gather_copy(p, 2, cols, me[axis], near(axis, 1), 2, n),
            gather_copy(p, 2, cols, me[axis], near(axis, 3), 2, n),
            gather_copy(p, 2, lo, (me[axis] + 3) % RING, near(axis, 1), 3, n + 6),
            gather_copy(p, 2, hi, (me[axis] + 1) % RING, near(axis, 3), 3, n + 6),
        ]

    g0 = [[gather_direct(k, p, 0) for p in range(3)] for k in range(GROUPS)]
    g1 = [[gather_direct(k, p, 1) for p in range(3)] for k in range(GROUPS)]
    g2 = [[gather_ring(k, p) for p in range(3)] for k in range(GROUPS)]

    def gathered(k, p, q):
        off, width, _ = PARTS[p][k]
        cols = pl.ds(off, width)
        like = (
            rb3.at[:, :, cols], rb2.at[:, :, :, cols], rb1.at[:, :, :, :, cols], ra1.at[:, :, :, cols]
        )[q]
        wait_for(like, g_recv.at[q * 6 + k * 3 + p])

    def start(copies):
        for c in copies:
            c.start()

    def grad_chunk(p, k, step):
        axis = GATHER[p][2]
        at = (me[axis] + step) % RING
        lhs = ht[p, at]
        off, width, _ = PARTS[p][k]
        cols = pl.ds(off, width)
        rhs = g[(*pick(GDIMS, {axis: at}), slice(None), cols)].reshape(256, width)
        part = jnp.dot(lhs, rhs, preferred_element_type=F32)
        if step == 0:
            acc[:, cols] = part
        else:
            acc[:, cols] += part

    for k in range(GROUPS):
        for p in range(3):
            start(g0[k][p])

    for c in local[3:6]:
        c.wait()
    old = old_v[...]
    ids = lax.broadcasted_iota(jnp.int32, old.shape, 0) * old.shape[1] + lax.broadcasted_iota(
        jnp.int32, old.shape, 1
    )
    new = old
    for i in range(drop.shape[1]):
        new = jnp.where(ids == drop[0, i], 0, new)
    for i in range(grow.shape[1]):
        new = jnp.where(ids == grow[0, i], 1, new)
    mask_ref[...] = new
    m[core] = jnp.zeros((8, BLK), F32)
    m[core, 0:2, 0 : old.shape[1]] = new.astype(F32)
    m[core, 2:4, 0 : old.shape[1]] = (new * old).astype(F32)
    swap[2].start()

    local[2].wait()
    swap[1].wait_recv()

    def sort_hidden(j, carry):
        for u in range(2):
            cols = pl.ds(pl.multiple_of(j * 2 * OWN + core * OWN + u * BLK, BLK), BLK)
            both = jnp.concatenate([hb[0, :, cols], hb[1, :, cols]], axis=0)
            t0[u, j // 16, j // 4 % 4, j % 4] = both
        return carry

    lax.fori_loop(0, 64, sort_hidden, 0)
    hid_start(0)

    def spread(t, carry):
        o = pl.multiple_of(t * BLK, BLK)
        block = lax.broadcasted_iota(jnp.int32, (BLK, BLK), 0) == core * (HALF // BLK) + t
        for i in range(2):
            expand[i, :, pl.ds(o, BLK)] = jnp.dot(
                m[i], block.astype(F32), preferred_element_type=F32
            )
        return carry

    def turn(i, carry):
        for p in range(3):
            sel = pick(GDIMS, {GATHER[p][2]: i})
            for n in range(4):
                part = h[(n // 2, n % 2, *sel)].reshape(256, BLK)
                ht[p, i, pl.ds(n * BLK, BLK), :] = part.T
        return carry

    for k in range(GROUPS):
        for p in range(3):
            gathered(k, p, 0)
            start(g1[k][p])
    hid_wait(0)
    hid_start(1)
    for p in range(3):
        gathered(0, p, 1)
        start(g2[0][p][:2])
    hid_wait(1)
    hid_start(2)
    for p in range(3):
        gathered(1, p, 1)
    local[7].wait()
    wait_for(xin.at[0:3, own_tokens], a_recv.at[3])
    swap[5].start()
    swap[2].wait_recv()
    lax.fori_loop(0, HALF // BLK, spread, 0)
    for p in range(3):
        gathered(0, p, 2)
        start(g2[0][p][2:])
        start(g2[1][p][:2])
    hid_wait(2)
    swap[4].start()
    swap[4].wait_recv()
    lax.fori_loop(0, RING, turn, 0)
    for k in range(GROUPS):
        for p in range(3):
            grad_chunk(p, k, 0)
    local[6].wait()
    swap[3].wait_recv()
    swap[5].wait_recv()

    def scatter_copy(p, q, v, cols, into, to, send, recv):
        fixed = {d: me[d] for d in SCATTER[p][:q]}
        fixed[SCATTER[p][q]] = v
        src = s.at[(*pick(SDIMS, fixed), slice(None), cols)]
        dst = into.at[(*([slice(None)] * (3 - q)), cols)]
        return remote(src, dst, s_send.at[send], s_recv.at[recv], to)

    def scatter_ring(k, p):
        off, width, half = PARTS[p][k]
        axis = SCATTER[p][0]
        lo, hi, n = pl.ds(off, half), pl.ds(off + half, width - half), k * 3 + p
        out = []
        for step, cols in ((1, lo), (3, hi)):
            v = (me[axis] + 2) % RING
            out.append(scatter_copy(p, 0, v, cols, ra1, near(axis, step), 0, n))
        for i, (step, cols) in enumerate(((1, hi), (3, lo), (1, lo), (3, hi))):
            v = (me[axis] + step) % RING
            out.append(scatter_copy(p, 0, v, cols, rb1.at[i % 2], near(axis, step), 1, 6 + n))
        return out

    def scatter_direct(k, p, q):
        off, width, _ = PARTS[p][k]
        axis = SCATTER[p][q]
        into, cols, n = (rb2, rb3)[q - 1], pl.ds(off, width), 6 + q * 6 + k * 3 + p
        return [
            scatter_copy(p, q, (me[axis] + d) % RING, cols, into.at[i], near(axis, d), 1 + q, n)
            for i, d in enumerate(FAR)
        ]

    s0 = [[scatter_ring(k, p) for p in range(3)] for k in range(GROUPS)]
    s1 = [[scatter_direct(k, p, 1) for p in range(3)] for k in range(GROUPS)]
    s2 = [[scatter_direct(k, p, 2) for p in range(3)] for k in range(GROUPS)]

    def scattered(k, p, q):
        off, width, _ = PARTS[p][k]
        cols = pl.ds(off, width)
        like = (
            ra1.at[:, :, :, cols], rb1.at[:, :, :, :, cols], rb2.at[:, :, :, cols], rb3.at[:, :, cols]
        )[q]
        wait_for(like, s_recv.at[q * 6 + k * 3 + p])

    def out_chunk(p, k, step):
        axis = SCATTER[p][0]
        sel = pick(SDIMS, {axis: (me[axis] + step) % RING})
        off, width, _ = PARTS[p][k]
        cols = pl.ds(off, width)
        part = jnp.dot(xin[sel].reshape(256, 2 * OWN), w[:, cols], preferred_element_type=F32)
        s[(*sel, slice(None), cols)] = part.astype(BF).reshape(RING, RING, ROWS, width)

    def update(p, k):
        off, width, _ = PARTS[p][k]
        cols = pl.ds(off, width)
        for r in range(4):
            side, row = r // 2, r % 2
            keep = expand[side, row : row + 1, cols]
            both = expand[side, row + 2 : row + 3, cols]
            span = pl.ds(r * BLK, BLK)
            w[span, cols] = (both * w[span, cols].astype(F32) - keep * acc[span, cols]).astype(BF)

    def add_into(p, q, v, cols, froms):
        fixed = {d: me[d] for d in SCATTER[p][:q]}
        fixed[SCATTER[p][q]] = v
        free = [d for d in SDIMS if d not in fixed]

        def one(lead):
            idx = dict(fixed)
            if free:
                idx[free[0]] = lead
            at = (*pick(SDIMS, idx), slice(None), cols)
            there = ((lead,) if free else ()) + (slice(None),) * (len(free) - 1 if free else 0)
            total = s[at].astype(F32)
            for ref, pre in froms:
                total = total + ref[(*pre, *there, slice(None), cols)].astype(F32)
            return at, total

        if not free:
            return one(None)[1]

        def step(i, carry):
            at, total = one(i)
            s[at] = total.astype(BF)
            return carry

        lax.fori_loop(0, RING, step, 0)
        return None

    def finish(k):
        for p in range(3):
            gathered(k, p, 3)
            grad_chunk(p, k, 2)
            update(p, k)
            out_chunk(p, k, 2)
            start(s0[k][p][:2])

    def sides(k):
        for p in range(3):
            out_chunk(p, k, 1)
            s0[k][p][2].start()
            out_chunk(p, k, 3)
            s0[k][p][3].start()

    def relay(k):
        for p in range(3):
            off, width, half = PARTS[p][k]
            scattered(k, p, 0)
            for i, cols in enumerate((pl.ds(off, half), pl.ds(off + half, width - half))):
                add_into(p, 0, (me[SCATTER[p][0]] + (1, 3)[i]) % RING, cols, [(ra1, ())])
                s0[k][p][4 + i].start()

    def settle(k):
        for p in range(3):
            off, width, _ = PARTS[p][k]
            scattered(k, p, 1)
            add_into(p, 0, me[SCATTER[p][0]], pl.ds(off, width), [(rb1, (0,)), (rb1, (1,))])
            start(s1[k][p])

    for p in range(3):
        grad_chunk(p, 0, 1)
        grad_chunk(p, 0, 3)
    finish(0)
    for p in range(3):
        gathered(1, p, 2)
        start(g2[1][p][2:])
    sides(0)
    for p in range(3):
        grad_chunk(p, 1, 1)
        grad_chunk(p, 1, 3)
    relay(0)
    finish(1)
    sides(1)
    for k in range(GROUPS):
        for p in range(3):
            out_chunk(p, k, 0)
    relay(1)
    settle(0)
    settle(1)
    for k in range(GROUPS):
        for p in range(3):
            off, width, _ = PARTS[p][k]
            scattered(k, p, 2)
            add_into(p, 1, me[SCATTER[p][1]], pl.ds(off, width), [(rb2, (i,)) for i in range(3)])
            start(s2[k][p])
    slot = fsdp % 8
    ends = []

    def deliver(k):
        base, shift = CHUNK * k // BLK * BLK, CHUNK * k % BLK
        piece = fin[:, pl.ds(base, PAD + BLK)]
        if shift:
            piece = pltpu.roll(piece, PAD + BLK - shift, 1)
        stage[k] = piece[:, :PAD].astype(BF)
        away = pltpu.make_async_remote_copy(
            src_ref=stage.at[k], dst_ref=land.at[slot], send_sem=f_send.at[k],
            recv_sem=f_recv.at[slot], device_id=last_dev(k), device_id_type=MESH,
        )

        @pl.when(jnp.logical_not(is_self(k)))
        def _():
            away.start()

        @pl.when(is_self(k))
        def _():
            pltpu.make_async_copy(stage.at[k], land.at[slot], f_recv.at[slot]).start()

        ends.append(away)

    fin[:, pl.ds(HALF, BLK)] = jnp.zeros((ROWS, BLK), F32)
    for k in range(GROUPS):
        for p in range(3):
            off, width, _ = PARTS[p][k]
            scattered(k, p, 3)
            total = add_into(p, 2, me[SCATTER[p][2]], pl.ds(off, width), [(rb3, (i,)) for i in range(3)])
            fin[:, pl.ds(off, width)] = total
        for n in range(4 * k, 4 * k + 4):
            deliver(n)
    for k in range(8):
        pltpu.make_async_copy(stage.at[k], land.at[k], f_recv.at[k]).wait()
        out_ref[pl.ds(k * ROWS, ROWS), :] = land[k][:, :CHUNK]

    for k in range(8):
        @pl.when(jnp.logical_not(is_self(k)))
        def _():
            ends[k].wait_send()
    for c in swap:
        c.wait_send()
    for i, like in enumerate((rb3, rb2, rb1, ra1)):
        wait_for(like, g_send.at[i])
    for i, like in enumerate((ra1, rb1, rb2, rb3)):
        wait_for(like, s_send.at[i])
    for i in range(3):
        wait_for(t0.at[:, 0:3], a_send.at[i])
    wait_for(xin.at[0:3, own_tokens], a_send.at[3])


def shards(hidden, grad_out, token_counts, weight, old_mask, drop_list, grow_list, inputs):
    inp = inputs.reshape(2, RING, ROWS, 2048)
    vmem = pl.BlockSpec(memory_space=pltpu.VMEM)
    hbm = pl.BlockSpec(memory_space=pl.ANY)
    dma = pltpu.SemaphoreType.DMA
    cube = (RING, RING, RING, ROWS)
    out, mask = pl.pallas_call(
        kernel,
        out_shape=(
            jax.ShapeDtypeStruct((128, CHUNK), BF),
            jax.ShapeDtypeStruct(old_mask.shape, jnp.int32),
        ),
        in_specs=[hbm] * 8,
        out_specs=(vmem, vmem),
        scratch_shapes=[
            pltpu.SMEM((1,), jnp.int32),
            pltpu.SMEM(drop_list.shape, jnp.int32),
            pltpu.SMEM(grow_list.shape, jnp.int32),
            pltpu.VMEM(old_mask.shape, jnp.int32),
            pltpu.VMEM((8, 2 * HALF), BF),
            pltpu.VMEM((8, 2 * HALF), BF),
            pltpu.VMEM((2, 8, HALF), BF),
            pltpu.VMEM((*cube, HALF), BF),
            pltpu.VMEM((2, 8, 64 * 2 * OWN), BF),
            pltpu.VMEM((2, *cube, BLK), BF),
            pltpu.VMEM((2, *cube, BLK), BF),
            pltpu.VMEM((2, *cube, BLK), BF),
            pltpu.VMEM((2, 2, *cube, BLK), BF),
            pltpu.VMEM((3, RING, 2 * OWN, 256), BF),
            pltpu.VMEM((2 * OWN, HALF), F32),
            pltpu.VMEM((2 * OWN, HALF), BF),
            pltpu.VMEM((*cube, 2 * OWN), BF),
            pltpu.VMEM((*cube, HALF), BF),
            pltpu.VMEM((2, 8, BLK), F32),
            pltpu.VMEM((2, 8, HALF), F32),
            pltpu.VMEM((RING, RING, ROWS, HALF), BF),
            pltpu.VMEM((2, RING, RING, ROWS, HALF), BF),
            pltpu.VMEM((3, RING, ROWS, HALF), BF),
            pltpu.VMEM((3, ROWS, HALF), BF),
            pltpu.VMEM((ROWS, HALF + BLK), F32),
            pltpu.VMEM((8, ROWS, PAD), BF),
            pltpu.VMEM((8, ROWS, PAD), BF),
            dma((4,)), dma((24,)), dma((4,)), dma((24,)), dma((6,)), dma((6,)),
            dma((8,)), dma((8,)), dma((4,)), dma((4,)), dma((14,)),
        ],
        compiler_params=pltpu.CompilerParams(
            collective_id=0, has_side_effects=True, vmem_limit_bytes=60 * 2**20
        ),
        cost_estimate=pl.CostEstimate(flops=8 * 10**9, bytes_accessed=10**7, transcendentals=0),
    )(token_counts, drop_list, grow_list, old_mask, grad_out, hidden, inp, weight)
    return (out, mask)


def solution(mesh):
    split = P(("fsdp", "grp"), None)
    return jax.shard_map(
        shards,
        mesh=mesh,
        in_specs=(split, split, P(("fsdp", "grp")), split, split, split, split, P("grp", "fsdp")),
        out_specs=(P("grp", "fsdp"), split),
        check_vma=False,
    )
```

```python
import jax
import jax.numpy as jnp
from jax import lax
from jax.experimental import pallas as pl
from jax.experimental.pallas import tpu as pltpu
from jax.sharding import PartitionSpec as P

MESH = pl.DeviceIdType.MESH
BF = jnp.bfloat16
F32 = jnp.float32

RING = 4
ROWS = 16
BLK = 128
HALF = 3712
OWN = 256
CHUNK = 464
PAD = 512

PARTS = (
    ((0, 640, 384), (2176, 512, 256)),
    ((640, 768, 384), (2688, 512, 256)),
    ((1408, 768, 384), (3200, 512, 256)),
)
GROUPS = 2
FAR = (1, 3, 2)
TURNS = (("x", "y", "z"), ("y", "z", "x"))
GATHER = (("x", "y", "z"), ("y", "z", "x"), ("z", "x", "y"))
SCATTER = (("z", "x", "y"), ("x", "y", "z"), ("y", "z", "x"))
GDIMS = ("x", "y", "z")
SDIMS = ("z", "x", "y")


def pick(dims, fixed):
    return tuple(fixed[d] if d in fixed else slice(None) for d in dims)


def kernel(
    count_ref, drop_ref, grow_ref, old_ref, grad_ref, hid_ref, inp_ref, w_ref,
    out_ref, mask_ref,
    count, drop, grow, old_v, grad, gm, gp, g, hb, t0, t1, t2, h, ht, acc, w, xin, s, m, expand, ra1, rb1, rb2, rb3, fin, stage,
    g_send, g_recv, s_send, s_recv, e_send, e_recv, f_send, f_recv, a_send, a_recv, loc,
):
    fsdp = lax.axis_index("fsdp")
    grp = lax.axis_index("grp")
    me = {"x": fsdp // RING, "y": fsdp % RING, "z": grp // 2}
    core = grp % 2

    def dev(x, y, z, c):
        return (x * RING + y, z * 2 + c)

    def near(axis, step):
        at = dict(me)
        at[axis] = (at[axis] + step) % RING
        return dev(at["x"], at["y"], at["z"], core)

    partner = dev(me["x"], me["y"], me["z"], 1 - core)

    bar = pltpu.get_barrier_semaphore()
    last_core = me["x"] // 2
    self_in = last_core == core
    own_k = (me["x"] % 2) * RING + me["y"]

    def last_dev(k):
        return dev(2 * core + k // RING, k % RING, me["z"], last_core)

    def is_self(k):
        return jnp.logical_and(self_in, own_k == k)

    for axis in ("x", "y", "z"):
        for step in FAR:
            pl.semaphore_signal(bar, inc=1, device_id=near(axis, step), device_id_type=MESH)
    pl.semaphore_signal(bar, inc=1, device_id=partner, device_id_type=MESH)
    mine = pl.ds(pl.multiple_of(core * HALF, BLK), HALF)
    other = pl.ds(pl.multiple_of((1 - core) * HALF, BLK), HALF)
    own_rows = pl.ds(pl.multiple_of(core * OWN, OWN), OWN)
    own_tokens = pl.ds(2 * core, 2)

    def slab(z):
        return pl.ds(pl.multiple_of(z * 2 * OWN, 2 * OWN), 2 * OWN)

    local = [
        pltpu.make_async_copy(*pair, loc.at[i])
        for i, pair in enumerate((
            (grad_ref, grad),
            (count_ref, count),
            (hid_ref, hb.at[core]),
            (old_ref, old_v),
            (drop_ref, drop),
            (grow_ref, grow),
            (w_ref.at[:, mine], w.at[own_rows, :]),
            (inp_ref.at[:, :, :, slab(me["z"])], xin.at[me["z"], own_tokens]),
        ))
    ]
    for c in local:
        c.start()

    def remote(src, dst, send, recv, to):
        return pltpu.make_async_remote_copy(
            src_ref=src, dst_ref=dst, send_sem=send, recv_sem=recv,
            device_id=to, device_id_type=MESH,
        )

    def wait_for(like, sem):
        pltpu.make_async_copy(like, like, sem).wait()

    local[0].wait()
    local[1].wait()
    rows = lax.broadcasted_iota(jnp.int32, grad.shape, 0)
    gm[...] = jnp.where(rows < count[0], grad[...].astype(F32), 0.0).astype(BF)
    gp[core] = gm[:, mine]
    pl.semaphore_wait(bar, 10)

    swap = [
        remote(gm.at[:, other], gp.at[core], e_send.at[0], e_recv.at[0], partner),
        remote(hid_ref, hb.at[core], e_send.at[1], e_recv.at[1], partner),
        remote(m.at[core], m.at[core], e_send.at[2], e_recv.at[2], partner),
        remote(w_ref.at[:, other], w.at[own_rows, :], e_send.at[3], e_recv.at[3], partner),
        remote(h.at[core], h.at[core], e_send.at[4], e_recv.at[4], partner),
        remote(xin.at[:, own_tokens], xin.at[:, own_tokens], e_send.at[5], e_recv.at[5], partner),
    ]
    swap[0].start()
    swap[1].start()
    swap[3].start()

    inp = [
        remote(
            inp_ref.at[:, :, :, slab((me["z"] + d) % RING)], xin.at[me["z"], own_tokens],
            a_send.at[3], a_recv.at[3], near("z", d),
        )
        for d in FAR
    ]
    hid = []
    for u in range(2):
        for q, axis in enumerate(TURNS[u]):
            src = (t0, t1, t2)[q].at[u]
            dst = (t1.at[u], t2.at[u], h.at[core, u])[q]

            def ends_of(d):
                v = (me[axis] + d) % RING
                return src.at[pick(GDIMS, {axis: v})], dst.at[pick(GDIMS, {axis: me[axis]})]

            stay = pltpu.make_async_copy(*ends_of(0), loc.at[8 + u * 3 + q])
            go = [remote(*ends_of(d), a_send.at[q], a_recv.at[q], near(axis, d)) for d in FAR]
            hid.append((stay, go))

    def hid_start(q):
        for u in range(2):
            for c in (*hid[u * 3 + q][1], hid[u * 3 + q][0]):
                c.start()

    def hid_wait(q):
        for u in range(2):
            hid[u * 3 + q][0].wait()
        wait_for(t0.at[:, 0:3], a_recv.at[q])

    for c in inp:
        c.start()
    swap[0].wait_recv()
    g[me["x"], me["y"], me["z"]] = jnp.concatenate([gp[0], gp[1]], axis=0)

    def gather_copy(p, q, cols, at, to, send, recv):
        fixed = {d: me[d] for d in GATHER[p][q:]}
        fixed[GATHER[p][q]] = at
        ref = g.at[(*pick(GDIMS, fixed), slice(None), cols)]
        return remote(ref, ref, g_send.at[send], g_recv.at[recv], to)

    def gather_direct(k, p, q):
        off, width, _ = PARTS[p][k]
        axis = GATHER[p][q]
        cols, n = pl.ds(off, width), q * 6 + k * 3 + p
        return [gather_copy(p, q, cols, me[axis], near(axis, d), q, n) for d in FAR]

    def gather_ring(k, p):
        off, width, half = PARTS[p][k]
        axis = GATHER[p][2]
        cols, lo, hi = pl.ds(off, width), pl.ds(off, half), pl.ds(off + half, width - half)
        n = 12 + k * 3 + p
        return [
            gather_copy(p, 2, cols, me[axis], near(axis, 1), 2, n),
            gather_copy(p, 2, cols, me[axis], near(axis, 3), 2, n),
            gather_copy(p, 2, lo, (me[axis] + 3) % RING, near(axis, 1), 3, n + 6),
            gather_copy(p, 2, hi, (me[axis] + 1) % RING, near(axis, 3), 3, n + 6),
        ]

    g0 = [[gather_direct(k, p, 0) for p in range(3)] for k in range(GROUPS)]
    g1 = [[gather_direct(k, p, 1) for p in range(3)] for k in range(GROUPS)]
    g2 = [[gather_ring(k, p) for p in range(3)] for k in range(GROUPS)]

    def gathered(k, p, q):
        off, width, _ = PARTS[p][k]
        cols = pl.ds(off, width)
        like = (
            rb3.at[:, :, cols], rb2.at[:, :, :, cols], rb1.at[:, :, :, :, cols], ra1.at[:, :, :, cols]
        )[q]
        wait_for(like, g_recv.at[q * 6 + k * 3 + p])

    def start(copies):
        for c in copies:
            c.start()

    def grad_chunk(p, k, step):
        axis = GATHER[p][2]
        at = (me[axis] + step) % RING
        lhs = ht[p, at]
        off, width, _ = PARTS[p][k]
        cols = pl.ds(off, width)
        rhs = g[(*pick(GDIMS, {axis: at}), slice(None), cols)].reshape(256, width)
        part = jnp.dot(lhs, rhs, preferred_element_type=F32)
        if step == 0:
            acc[:, cols] = part
        else:
            acc[:, cols] += part

    for k in range(GROUPS):
        for p in range(3):
            start(g0[k][p])

    for c in local[3:6]:
        c.wait()
    old = old_v[...]
    ids = lax.broadcasted_iota(jnp.int32, old.shape, 0) * old.shape[1] + lax.broadcasted_iota(
        jnp.int32, old.shape, 1
    )
    new = old
    for i in range(drop.shape[1]):
        new = jnp.where(ids == drop[0, i], 0, new)
    for i in range(grow.shape[1]):
        new = jnp.where(ids == grow[0, i], 1, new)
    mask_ref[...] = new
    m[core] = jnp.zeros((8, BLK), F32)
    m[core, 0:2, 0 : old.shape[1]] = new.astype(F32)
    m[core, 2:4, 0 : old.shape[1]] = (new * old).astype(F32)
    swap[2].start()

    local[2].wait()
    swap[1].wait_recv()

    def sort_hidden(j, carry):
        for u in range(2):
            cols = pl.ds(pl.multiple_of(j * 2 * OWN + core * OWN + u * BLK, BLK), BLK)
            both = jnp.concatenate([hb[0, :, cols], hb[1, :, cols]], axis=0)
            t0[u, j // 16, j // 4 % 4, j % 4] = both
        return carry

    lax.fori_loop(0, 64, sort_hidden, 0)
    hid_start(0)

    def spread(t, carry):
        o = pl.multiple_of(t * BLK, BLK)
        block = lax.broadcasted_iota(jnp.int32, (BLK, BLK), 0) == core * (HALF // BLK) + t
        for i in range(2):
            expand[i, :, pl.ds(o, BLK)] = jnp.dot(
                m[i], block.astype(F32), preferred_element_type=F32
            )
        return carry

    def turn(i, carry):
        for p in range(3):
            sel = pick(GDIMS, {GATHER[p][2]: i})
            for n in range(4):
                part = h[(n // 2, n % 2, *sel)].reshape(256, BLK)
                ht[p, i, pl.ds(n * BLK, BLK), :] = part.T
        return carry

    for k in range(GROUPS):
        for p in range(3):
            gathered(k, p, 0)
            start(g1[k][p])
    hid_wait(0)
    hid_start(1)
    for p in range(3):
        gathered(0, p, 1)
        start(g2[0][p][:2])
    hid_wait(1)
    hid_start(2)
    for p in range(3):
        gathered(1, p, 1)
    local[7].wait()
    wait_for(xin.at[0:3, own_tokens], a_recv.at[3])
    swap[5].start()
    swap[2].wait_recv()
    lax.fori_loop(0, HALF // BLK, spread, 0)
    for p in range(3):
        gathered(0, p, 2)
        start(g2[0][p][2:])
        start(g2[1][p][:2])
    hid_wait(2)
    swap[4].start()
    swap[4].wait_recv()
    lax.fori_loop(0, RING, turn, 0)
    for k in range(GROUPS):
        for p in range(3):
            grad_chunk(p, k, 0)
    local[6].wait()
    swap[3].wait_recv()
    swap[5].wait_recv()

    def scatter_copy(p, q, v, cols, into, to, send, recv):
        fixed = {d: me[d] for d in SCATTER[p][:q]}
        fixed[SCATTER[p][q]] = v
        src = s.at[(*pick(SDIMS, fixed), slice(None), cols)]
        dst = into.at[(*([slice(None)] * (3 - q)), cols)]
        return remote(src, dst, s_send.at[send], s_recv.at[recv], to)

    def scatter_ring(k, p):
        off, width, half = PARTS[p][k]
        axis = SCATTER[p][0]
        lo, hi, n = pl.ds(off, half), pl.ds(off + half, width - half), k * 3 + p
        out = []
        for step, cols in ((1, lo), (3, hi)):
            v = (me[axis] + 2) % RING
            out.append(scatter_copy(p, 0, v, cols, ra1, near(axis, step), 0, n))
        for i, (step, cols) in enumerate(((1, hi), (3, lo), (1, lo), (3, hi))):
            v = (me[axis] + step) % RING
            out.append(scatter_copy(p, 0, v, cols, rb1.at[i % 2], near(axis, step), 1, 6 + n))
        return out

    def scatter_direct(k, p, q):
        off, width, _ = PARTS[p][k]
        axis = SCATTER[p][q]
        into, cols, n = (rb2, rb3)[q - 1], pl.ds(off, width), 6 + q * 6 + k * 3 + p
        return [
            scatter_copy(p, q, (me[axis] + d) % RING, cols, into.at[i], near(axis, d), 1 + q, n)
            for i, d in enumerate(FAR)
        ]

    s0 = [[scatter_ring(k, p) for p in range(3)] for k in range(GROUPS)]
    s1 = [[scatter_direct(k, p, 1) for p in range(3)] for k in range(GROUPS)]
    s2 = [[scatter_direct(k, p, 2) for p in range(3)] for k in range(GROUPS)]

    def scattered(k, p, q):
        off, width, _ = PARTS[p][k]
        cols = pl.ds(off, width)
        like = (
            ra1.at[:, :, :, cols], rb1.at[:, :, :, :, cols], rb2.at[:, :, :, cols], rb3.at[:, :, cols]
        )[q]
        wait_for(like, s_recv.at[q * 6 + k * 3 + p])

    def out_chunk(p, k, step):
        axis = SCATTER[p][0]
        sel = pick(SDIMS, {axis: (me[axis] + step) % RING})
        off, width, _ = PARTS[p][k]
        cols = pl.ds(off, width)
        part = jnp.dot(xin[sel].reshape(256, 2 * OWN), w[:, cols], preferred_element_type=F32)
        s[(*sel, slice(None), cols)] = part.astype(BF).reshape(RING, RING, ROWS, width)

    def update(p, k):
        off, width, _ = PARTS[p][k]
        cols = pl.ds(off, width)
        for r in range(4):
            side, row = r // 2, r % 2
            keep = expand[side, row : row + 1, cols]
            both = expand[side, row + 2 : row + 3, cols]
            span = pl.ds(r * BLK, BLK)
            w[span, cols] = (both * w[span, cols].astype(F32) - keep * acc[span, cols]).astype(BF)

    def add_into(p, q, v, cols, froms):
        fixed = {d: me[d] for d in SCATTER[p][:q]}
        fixed[SCATTER[p][q]] = v
        free = [d for d in SDIMS if d not in fixed]

        def one(lead):
            idx = dict(fixed)
            if free:
                idx[free[0]] = lead
            at = (*pick(SDIMS, idx), slice(None), cols)
            there = ((lead,) if free else ()) + (slice(None),) * (len(free) - 1 if free else 0)
            total = s[at].astype(F32)
            for ref, pre in froms:
                total = total + ref[(*pre, *there, slice(None), cols)].astype(F32)
            return at, total

        if not free:
            return one(None)[1]

        def step(i, carry):
            at, total = one(i)
            s[at] = total.astype(BF)
            return carry

        lax.fori_loop(0, RING, step, 0)
        return None

    def finish(k):
        for p in range(3):
            gathered(k, p, 3)
            grad_chunk(p, k, 2)
            update(p, k)
            out_chunk(p, k, 2)
            start(s0[k][p][:2])

    def sides(k):
        for p in range(3):
            out_chunk(p, k, 1)
            s0[k][p][2].start()
            out_chunk(p, k, 3)
            s0[k][p][3].start()

    def relay(k):
        for p in range(3):
            off, width, half = PARTS[p][k]
            scattered(k, p, 0)
            for i, cols in enumerate((pl.ds(off, half), pl.ds(off + half, width - half))):
                add_into(p, 0, (me[SCATTER[p][0]] + (1, 3)[i]) % RING, cols, [(ra1, ())])
                s0[k][p][4 + i].start()

    def settle(k):
        for p in range(3):
            off, width, _ = PARTS[p][k]
            scattered(k, p, 1)
            add_into(p, 0, me[SCATTER[p][0]], pl.ds(off, width), [(rb1, (0,)), (rb1, (1,))])
            start(s1[k][p])

    for p in range(3):
        grad_chunk(p, 0, 1)
        grad_chunk(p, 0, 3)
    finish(0)
    for p in range(3):
        gathered(1, p, 2)
        start(g2[1][p][2:])
    sides(0)
    for p in range(3):
        grad_chunk(p, 1, 1)
        grad_chunk(p, 1, 3)
    relay(0)
    finish(1)
    sides(1)
    for k in range(GROUPS):
        for p in range(3):
            out_chunk(p, k, 0)
    relay(1)
    settle(0)
    settle(1)
    for k in range(GROUPS):
        for p in range(3):
            off, width, _ = PARTS[p][k]
            scattered(k, p, 2)
            add_into(p, 1, me[SCATTER[p][1]], pl.ds(off, width), [(rb2, (i,)) for i in range(3)])
            start(s2[k][p])
    slot = fsdp % 8
    ends = []

    def deliver(k):
        base, shift = CHUNK * k // BLK * BLK, CHUNK * k % BLK
        piece = fin[:, pl.ds(base, PAD + BLK)]
        if shift:
            piece = pltpu.roll(piece, PAD + BLK - shift, 1)
        stage[k] = piece[:, :PAD].astype(BF)
        away = pltpu.make_async_remote_copy(
            src_ref=stage.at[k], dst_ref=out_ref.at[slot], send_sem=f_send.at[k],
            recv_sem=f_recv.at[slot], device_id=last_dev(k), device_id_type=MESH,
        )

        @pl.when(jnp.logical_not(is_self(k)))
        def _():
            away.start()

        @pl.when(is_self(k))
        def _():
            pltpu.make_async_copy(stage.at[k], out_ref.at[slot], f_recv.at[slot]).start()

        ends.append(away)

    fin[:, pl.ds(HALF, BLK)] = jnp.zeros((ROWS, BLK), F32)
    for k in range(GROUPS):
        for p in range(3):
            off, width, _ = PARTS[p][k]
            scattered(k, p, 3)
            total = add_into(p, 2, me[SCATTER[p][2]], pl.ds(off, width), [(rb3, (i,)) for i in range(3)])
            fin[:, pl.ds(off, width)] = total
        for n in range(4 * k, 4 * k + 4):
            deliver(n)
    for k in range(8):
        pltpu.make_async_copy(stage.at[k], out_ref.at[k], f_recv.at[k]).wait()

    for k in range(8):
        @pl.when(jnp.logical_not(is_self(k)))
        def _():
            ends[k].wait_send()
    for c in swap:
        c.wait_send()
    for i, like in enumerate((rb3, rb2, rb1, ra1)):
        wait_for(like, g_send.at[i])
    for i, like in enumerate((ra1, rb1, rb2, rb3)):
        wait_for(like, s_send.at[i])
    for i in range(3):
        wait_for(t0.at[:, 0:3], a_send.at[i])
    wait_for(xin.at[0:3, own_tokens], a_send.at[3])


def shards(hidden, grad_out, token_counts, weight, old_mask, drop_list, grow_list, inputs):
    inp = inputs.reshape(2, RING, ROWS, 2048)
    vmem = pl.BlockSpec(memory_space=pltpu.VMEM)
    hbm = pl.BlockSpec(memory_space=pl.ANY)
    dma = pltpu.SemaphoreType.DMA
    cube = (RING, RING, RING, ROWS)
    out, mask = pl.pallas_call(
        kernel,
        out_shape=(
            jax.ShapeDtypeStruct((8, ROWS, PAD), BF),
            jax.ShapeDtypeStruct(old_mask.shape, jnp.int32),
        ),
        in_specs=[hbm] * 8,
        out_specs=(vmem, vmem),
        scratch_shapes=[
            pltpu.SMEM((1,), jnp.int32),
            pltpu.SMEM(drop_list.shape, jnp.int32),
            pltpu.SMEM(grow_list.shape, jnp.int32),
            pltpu.VMEM(old_mask.shape, jnp.int32),
            pltpu.VMEM((8, 2 * HALF), BF),
            pltpu.VMEM((8, 2 * HALF), BF),
            pltpu.VMEM((2, 8, HALF), BF),
            pltpu.VMEM((*cube, HALF), BF),
            pltpu.VMEM((2, 8, 64 * 2 * OWN), BF),
            pltpu.VMEM((2, *cube, BLK), BF),
            pltpu.VMEM((2, *cube, BLK), BF),
            pltpu.VMEM((2, *cube, BLK), BF),
            pltpu.VMEM((2, 2, *cube, BLK), BF),
            pltpu.VMEM((3, RING, 2 * OWN, 256), BF),
            pltpu.VMEM((2 * OWN, HALF), F32),
            pltpu.VMEM((2 * OWN, HALF), BF),
            pltpu.VMEM((*cube, 2 * OWN), BF),
            pltpu.VMEM((*cube, HALF), BF),
            pltpu.VMEM((2, 8, BLK), F32),
            pltpu.VMEM((2, 8, HALF), F32),
            pltpu.VMEM((RING, RING, ROWS, HALF), BF),
            pltpu.VMEM((2, RING, RING, ROWS, HALF), BF),
            pltpu.VMEM((3, RING, ROWS, HALF), BF),
            pltpu.VMEM((3, ROWS, HALF), BF),
            pltpu.VMEM((ROWS, HALF + BLK), F32),
            pltpu.VMEM((8, ROWS, PAD), BF),
            dma((4,)), dma((24,)), dma((4,)), dma((24,)), dma((6,)), dma((6,)),
            dma((8,)), dma((8,)), dma((4,)), dma((4,)), dma((14,)),
        ],
        compiler_params=pltpu.CompilerParams(
            collective_id=0, has_side_effects=True, vmem_limit_bytes=60 * 2**20
        ),
        cost_estimate=pl.CostEstimate(flops=8 * 10**9, bytes_accessed=10**7, transcendentals=0),
    )(token_counts, drop_list, grow_list, old_mask, grad_out, hidden, inp, weight)
    return (out.reshape(128, PAD)[:, :CHUNK], mask)


def solution(mesh):
    split = P(("fsdp", "grp"), None)
    return jax.shard_map(
        shards,
        mesh=mesh,
        in_specs=(split, split, P(("fsdp", "grp")), split, split, split, split, P("grp", "fsdp")),
        out_specs=(P("grp", "fsdp"), split),
        check_vma=False,
    )
```
